256 devices in a mesh: ctx: 16 (over z, y_lo), exp: 16 (over x, y_hi, core).
Axes of the slice: x: 4, y: 4 (y_hi: 2, y_lo: 2; y = y_hi * 2 + y_lo), z: 8, core: 2. Of those that a mesh axis runs over, the one named last changes fastest.
Arguments:
- query_rows: bfloat16 [16, 1024, 2560], P('exp', 'ctx'), may hold values from -8 to 8
- stretch_keys: bfloat16 [16, 1024, 512], P('exp', 'ctx'), may hold values from -4 to 4
- stretch_values: bfloat16 [16, 1024, 512], P('exp', 'ctx'), may hold values from -4 to 4
- cache_keys: bfloat16 [16, 4096, 512], P('exp', 'ctx'), may hold values from -4 to 4
- cache_values: bfloat16 [16, 4096, 512], P('exp', 'ctx'), may hold values from -4 to 4
- cache_len: int32 [16], P('exp'), may hold values from 1024 to 4096, as said below
- residual: bfloat16 [16, 1024, 2560], P(None, 'ctx', 'exp'), may hold values from -15 to 15
- out_weight: bfloat16 [2560, 2560], P(None, 'exp'), may hold values from -0.125 to 0.125
- norm_gain: bfloat16 [2560], replicated, may hold values from 0.099609375 to 1.8984375
- router_weight: bfloat16 [2560, 32], P(None, 'exp'), may hold values from -0.125 to 0.125
- expert_ids: int32 [16, 1024, 1], replicated, may hold values from 0 to 31; in each aligned block of 64 rows (0 to 63, 64 to 127, ..., all dimensions but the last counted through in order) at most 3 rows name the same one
- gate_weight: bfloat16 [32, 2560, 4096], P('exp', None, 'ctx'), may hold values from -0.125 to 0.125
- up_weight: bfloat16 [32, 2560, 4096], P('exp', None, 'ctx'), may hold values from -0.125 to 0.125
- down_weight: bfloat16 [32, 4096, 2560], P('exp', 'ctx'), may hold values from -0.09375 to 0.09375
Outputs:
- layer_out: bfloat16 [16, 1024, 2560], P(None, 'ctx', 'exp')
The draws below stay inside these ranges and needn't reach their ends.
Inputs may be any that keep to these rules, and one draw needn't show every extreme that they name: The first cache_len[b] cache slots of sequence b hold its earlier tokens and the stretch follows them; some sequence fills all 4096 slots and some holds exactly 1024. `expert_ids`: within each sequence, the tokens of each aligned block of 64 stretch positions name any one expert at most 3 times.
All inputs are finite; a program needn't handle non-finite values.
Results may differ from the reference program's by a relative error of at most 0.009.
Values may be sent and summed in bfloat16 or wider, within the bound.
No kernel may reach another device: no remote copies, remote signals or barrier semaphores. Data moves between devices by JAX's collectives and lax.ppermute only.
A program may use at most 128 MiB of HBM per device.

```python
import math
import jax
import jax.numpy as jnp
import numpy as np
from jax import lax

D = 2560
HEADS = 20
KV_HEADS = 4
HEAD_DIM = 128
FF = 4096
STRETCH_DEV = 64
SEQS = 16
STRETCH = 1024
CACHE = 4096
EXPERTS = 32
FF_BLOCK = 256
CAP = 3
N_CTX = 16


def draw_query_rows(key, part):
    key = jax.random.fold_in(key, 11)
    base = jnp.clip(jax.random.normal(key, (SEQS, STRETCH, HEADS * HEAD_DIM), jnp.float32), -4.0, 4.0)
    return base.astype(jnp.bfloat16)


def draw_cache_keys(key, part):
    key = jax.random.fold_in(key, 12)
    base = jnp.clip(jax.random.normal(key, (SEQS, CACHE, KV_HEADS * HEAD_DIM), jnp.float32), -4.0, 4.0)
    return base.astype(jnp.bfloat16)


def draw_cache_len(key, part):
    key = jax.random.fold_in(key, 13)
    first_key, second_key = jax.random.split(key)
    lengths = jax.random.randint(first_key, (SEQS,), CACHE // 4, CACHE + 1)
    spot = jax.random.randint(second_key, (), 0, SEQS)
    lengths = lengths.at[spot].set(CACHE)
    lengths = lengths.at[(spot + 1) % SEQS].set(CACHE // 4)
    return lengths.astype(jnp.int32)


def draw_residual(key, part):
    key = jax.random.fold_in(key, 14)
    first_key = jax.random.fold_in(key, 0)
    base = jnp.clip(jax.random.normal(first_key, (SEQS, STRETCH, D), jnp.float32), -4.0, 4.0)
    base = 0.5 * base
    return base.astype(jnp.bfloat16)


def block_scale(key, dims, cuts, low, high):
    factor_of, own = 1.0, jax.random.fold_in(key, 6)
    for position, shards_of in cuts:
        steps = jnp.exp(jax.random.uniform(jax.random.fold_in(own, position), (shards_of,), jnp.float32, low / len(cuts), high / len(cuts)))
        factor_of = factor_of * jnp.repeat(steps, dims[position] // shards_of).reshape([-1 if axis == position else 1 for axis in range(len(dims))])
    return factor_of


def deal_out(stream_key, own, number, rows, amount, top, limit, lean):
    ranking = jax.random.permutation(stream_key, amount)
    heavy_load, ordinary = shares(amount, rows * top, limit, lean, True), shares(amount, rows * top, limit, lean, False)
    places = jnp.arange(amount)

    def named(sizes, offset_by):
        used = int((sizes > 0).sum())
        fixed = max(1, used // 4)
        shifted = fixed + (places - fixed + offset_by * (used - fixed)) % max(1, amount - fixed)
        return jnp.zeros((amount,), jnp.int32).at[ranking[jnp.where(places < fixed, places, shifted)]].set(jnp.asarray(sizes, jnp.int32))

    sizes = jnp.where(number % 4 == 0, named(heavy_load, number // 4), named(ordinary, number - number // 4 - 1))
    mixed = jax.random.permutation(jax.random.fold_in(own, 3), amount)
    giver, receiver = mixed[0:amount // 2 * 2:2], mixed[1:amount // 2 * 2:2]
    margin = jnp.minimum(sizes[giver] - 1, limit - sizes[receiver]) // 2
    margin = jnp.where((giver == ranking[0]) | (receiver == ranking[0]) | (sizes[receiver] == 0), 0, jnp.maximum(margin, 0))
    shifted = jax.random.randint(jax.random.fold_in(own, 4), (amount // 2,), 0, 1 << 20) % (margin + 1)
    sizes = sizes.at[giver].add(-shifted).at[receiver].add(shifted)
    items = jnp.searchsorted(jnp.cumsum(sizes), jnp.arange(rows * top), side="right").astype(jnp.int32)
    table = items.reshape(top, rows).T
    table = table[jax.random.permutation(jax.random.fold_in(own, 1), rows)]
    offset_by = jax.random.randint(jax.random.fold_in(own, 2), (rows, 1), 0, top)
    return jnp.take_along_axis(table, (jnp.arange(top)[None, :] + offset_by) % top, axis=1)


def shares(amount, total, reach, slope, full):
    weights = [(1 << 20) // math.isqrt(rank ** slope) + 1 for rank in range(1, amount + 1)]
    largest = reach if full else min(reach, max(-(-total // amount), total * weights[0] // sum(weights)))
    least = 1 if total - largest >= amount - 1 else 0
    counts, surplus = [largest] + [least] * (amount - 1), total - largest - least * (amount - 1)
    while surplus > 0:
        free = [i for i in range(1, amount) if counts[i] < largest] or [i for i in range(1, amount) if counts[i] < reach]
        mass, budget = sum([weights[i] for i in free]), surplus
        for i in free:
            addition = min(reach - counts[i], max(1, budget * weights[i] // mass), surplus)
            counts[i] = counts[i] + addition
            surplus = surplus - addition
    return np.array(counts)


def centred(stream_key, extent, spread, bound, pieces=(), kind=jnp.bfloat16):
    level = block_scale(stream_key, extent, pieces, -0.22, 0.18) if pieces else 1.0
    entries = jax.random.normal(stream_key, extent, jnp.float32) * spread * level
    return jnp.minimum(jnp.maximum(entries, -bound), bound).astype(kind)


def setup_inputs(seed: int = 0) -> dict:
    seeds = jax.random.split(jax.random.key(seed), 15)
    query_rows = draw_query_rows(jax.random.fold_in(seeds[14], 71), 0)
    stretch_keys = centred(seeds[1], (SEQS, STRETCH, KV_HEADS * HEAD_DIM), 1.0, 4.0, ((0, 16), (1, 16)))
    stretch_values = centred(seeds[2], (SEQS, STRETCH, KV_HEADS * HEAD_DIM), 1.0, 4.0, ((0, 16), (1, 16)))
    cache_keys = draw_cache_keys(jax.random.fold_in(seeds[14], 71), 0)
    cache_values = centred(seeds[4], (SEQS, CACHE, KV_HEADS * HEAD_DIM), 1.0, 4.0, ((0, 16), (1, 16)))
    cache_len = draw_cache_len(jax.random.fold_in(seeds[14], 71), 0)
    residual = draw_residual(jax.random.fold_in(seeds[14], 71), 0)
    out_weight = centred(seeds[7], (HEADS * HEAD_DIM, D), (HEADS * HEAD_DIM) ** -0.5, 0.125, ((1, 16),))
    norm_gain = jnp.clip(1.0 + 0.18 * jax.random.normal(seeds[8], (D,), jnp.float32), 0.099609375, 1.8984375).astype(jnp.bfloat16)
    router_weight = centred(seeds[9], (D, EXPERTS), D ** -0.5, 0.125, ((1, 16),))
    expert_ids_keys = jax.random.split(jax.random.fold_in(seeds[10], 1), SEQS * STRETCH // STRETCH_DEV)
    expert_ids_turns = jax.random.permutation(jax.random.fold_in(seeds[10], 3), SEQS * STRETCH // STRETCH_DEV)
    expert_ids = jax.vmap(lambda own, number: deal_out(jax.random.fold_in(seeds[10], 2), own, number, STRETCH_DEV, EXPERTS, 1, CAP, 2))(expert_ids_keys, expert_ids_turns).reshape((SEQS, STRETCH, 1))
    gate_weight = centred(seeds[11], (EXPERTS, D, FF), D ** -0.5, 0.125, ((0, 16), (2, 16)))
    up_weight = centred(seeds[12], (EXPERTS, D, FF), D ** -0.5, 0.125, ((0, 16), (2, 16)))
    down_weight = centred(seeds[13], (EXPERTS, FF, D), FF ** -0.5, 0.09375, ((0, 16), (1, 16)))
    return dict(query_rows=query_rows, stretch_keys=stretch_keys, stretch_values=stretch_values, cache_keys=cache_keys, cache_values=cache_values, cache_len=cache_len, residual=residual, out_weight=out_weight, norm_gain=norm_gain, router_weight=router_weight, expert_ids=expert_ids, gate_weight=gate_weight, up_weight=up_weight, down_weight=down_weight)


NEG_FILL = -1e+30
EPSILON = 1e-05

def to_bf16_and_back(numbers):
    rounded = numbers.astype(jnp.bfloat16)
    rounded = lax.optimization_barrier(rounded)
    return rounded.astype(jnp.float32)

def attend_head(queries, key_block, value_block, length):
    scores = jnp.einsum('cgd,kd->gck', queries, key_block, precision=lax.Precision.HIGHEST) / math.sqrt(HEAD_DIM)
    slot_index = jnp.arange(CACHE + STRETCH)
    places = jnp.arange(STRETCH)
    alive_mask = jnp.where(slot_index[None, :] < CACHE, slot_index[None, :] < length, slot_index[None, :] - CACHE <= places[:, None])
    scores = jnp.where(alive_mask[None], scores, NEG_FILL)
    highest = lax.optimization_barrier(jnp.max(scores, axis=-1, keepdims=True))
    weights = jnp.where(alive_mask[None], jnp.exp(scores - highest), 0.0)
    totals = lax.optimization_barrier(jnp.sum(weights, axis=-1))
    mixture = jnp.einsum('gck,kd->gcd', to_bf16_and_back(weights), value_block, precision=lax.Precision.HIGHEST)
    return mixture / totals[..., None]

def attend_sequence(operands):
    queries, key_rows, value_rows, length = operands
    group_size = HEADS // KV_HEADS
    query_float = queries.astype(jnp.float32).reshape(STRETCH, KV_HEADS, group_size, HEAD_DIM)
    key_float = key_rows.astype(jnp.float32).reshape(CACHE + STRETCH, KV_HEADS, HEAD_DIM)
    value_float = value_rows.astype(jnp.float32).reshape(CACHE + STRETCH, KV_HEADS, HEAD_DIM)

    def one_head(head_index):
        return attend_head(query_float[:, head_index], key_float[:, head_index], value_float[:, head_index], length)
    heads_out = lax.map(one_head, jnp.arange(KV_HEADS))
    return jnp.transpose(heads_out, (2, 0, 1, 3)).reshape(STRETCH, HEADS * HEAD_DIM).astype(jnp.bfloat16)

def run_expert(operands):
    rows_in, gate_matrix, up_matrix, down_matrix = operands
    rows_float = rows_in.astype(jnp.float32)
    gate_part = jnp.dot(rows_float, gate_matrix.astype(jnp.float32), precision=lax.Precision.HIGHEST)
    up_part = jnp.dot(rows_float, up_matrix.astype(jnp.float32), precision=lax.Precision.HIGHEST)
    activation = to_bf16_and_back(jax.nn.silu(gate_part) * up_part)
    slot_total = rows_in.shape[0]
    blocks = activation.reshape(slot_total, N_CTX, FF_BLOCK)
    down_blocks = down_matrix.astype(jnp.float32).reshape(N_CTX, FF_BLOCK, D)
    partials = jnp.einsum('snf,nfd->nsd', blocks, down_blocks, precision=lax.Precision.HIGHEST)
    return lax.optimization_barrier(jnp.sum(to_bf16_and_back(partials), axis=0)).astype(jnp.bfloat16)

def reference(query_rows, stretch_keys, stretch_values, cache_keys, cache_values, cache_len, residual, out_weight, norm_gain, router_weight, expert_ids, gate_weight, up_weight, down_weight):
    key_rows = jnp.concatenate([cache_keys, stretch_keys], axis=1)
    value_rows = jnp.concatenate([cache_values, stretch_values], axis=1)
    attended = lax.map(attend_sequence, (query_rows, key_rows, value_rows, cache_len))
    token_count = SEQS * STRETCH
    projected = jnp.dot(attended.reshape(token_count, HEADS * HEAD_DIM), out_weight, preferred_element_type=jnp.float32)
    hidden = (residual.reshape(token_count, D).astype(jnp.float32) + projected).astype(jnp.bfloat16)
    hidden_float = hidden.astype(jnp.float32)
    mean_square = lax.optimization_barrier(jnp.mean(hidden_float * hidden_float, axis=-1, keepdims=True))
    normed = hidden_float * lax.rsqrt(mean_square + EPSILON) * norm_gain.astype(jnp.float32)
    logits = jnp.dot(normed, router_weight.astype(jnp.float32), precision=lax.Precision.HIGHEST)
    flat_ids = expert_ids.reshape(token_count).astype(jnp.int32)
    chosen = jnp.take_along_axis(logits, flat_ids[:, None], axis=1)
    routed = (jax.nn.sigmoid(chosen) * normed).astype(jnp.bfloat16)
    member = (flat_ids[:, None] == jnp.arange(EXPERTS, dtype=jnp.int32)[None, :]).astype(jnp.int32)
    slot_ranks = lax.optimization_barrier(jnp.sum((jnp.cumsum(member, axis=0) - 1) * member, axis=1)).astype(jnp.int32)
    slot_total = CAP * SEQS * N_CTX
    buffers = jnp.zeros((EXPERTS, slot_total, D), jnp.bfloat16).at[flat_ids, slot_ranks].set(routed)
    results = lax.map(run_expert, (buffers, gate_weight, up_weight, down_weight))
    expert_out = results[flat_ids, slot_ranks]
    combined = hidden_float + expert_out.astype(jnp.float32)
    return combined.astype(jnp.bfloat16).reshape(SEQS, STRETCH, D)
```

```python
import functools
import math

import jax
import jax.numpy as jnp
from jax import lax
from jax.experimental import pallas as pl
from jax.experimental.pallas import tpu as pltpu
from jax.sharding import Mesh, PartitionSpec as P

HEADS = 20
KV_HEADS = 4
HEAD_DIM = 128
GROUP = HEADS // KV_HEADS
CAP = 3
EPSILON = 1e-05
FAR = 1 << 30
FILL = -1e30
LOW = -1e20
E_AXES = ("x", "yh", "c")
PLANE = ("x", "yh", "c", "yl")
F32 = jnp.float32
BF16 = jnp.bfloat16


def attend_kernel(pieces, first, last, *refs):
    q_ref, place_ref = refs[0], refs[1]
    key_refs = refs[2 : 2 + pieces]
    value_refs = refs[2 + pieces : 2 + 2 * pieces]
    rest = refs[2 + 2 * pieces :]
    if not first:
        m_in, l_in, a_in = rest[:3]
        rest = rest[3:]
    rows = q_ref.shape[0]
    pair = q_ref.shape[1] // (GROUP * HEAD_DIM)
    factor = math.log2(math.e) / math.sqrt(HEAD_DIM)
    own = lax.broadcasted_iota(jnp.int32, (GROUP * rows, 1), 0) % rows
    for j in range(pair):
        queries = jnp.concatenate(
            [
                q_ref[:, (j * GROUP + g) * HEAD_DIM : (j * GROUP + g + 1) * HEAD_DIM]
                for g in range(GROUP)
            ],
            axis=0,
        )
        lanes = slice(j * HEAD_DIM, (j + 1) * HEAD_DIM)
        scores = []
        for i in range(pieces):
            s = lax.dot_general(
                queries,
                key_refs[i][:, lanes],
                (((1,), (1,)), ((), ())),
                preferred_element_type=F32,
            )
            scores.append(jnp.where(place_ref[i] <= own, s * factor, FILL))
        top = functools.reduce(
            jnp.maximum, [jnp.max(s, axis=-1, keepdims=True) for s in scores]
        )
        if first:
            m_new = jnp.maximum(top, LOW)
        else:
            m_old = m_in[j]
            m_new = jnp.maximum(m_old, top)
            alpha = jnp.exp2(m_old - m_new)
        high = m_new[:, :1]
        total = 0.0
        summed = 0.0
        for i in range(pieces):
            p = jnp.exp2(scores[i] - high)
            total = total + jnp.sum(p, axis=-1, keepdims=True)
            summed = summed + jnp.dot(
                p.astype(BF16), value_refs[i][:, lanes], preferred_element_type=F32
            )
        if not first:
            total = l_in[j] * alpha + total
            summed = a_in[j] * alpha + summed
        if last:
            result = (summed / total).astype(BF16)
            for g in range(GROUP):
                rest[0][:, (j * GROUP + g) * HEAD_DIM : (j * GROUP + g + 1) * HEAD_DIM] = result[
                    g * rows : (g + 1) * rows
                ]
        else:
            shape = (GROUP * rows, HEAD_DIM)
            rest[0][j] = jnp.broadcast_to(m_new, shape)
            rest[1][j] = jnp.broadcast_to(total, shape)
            rest[2][j] = summed


def attend(queries, places, keys, values, state, last):
    pieces = len(keys)
    rows, width = queries.shape
    pair = width // (GROUP * HEAD_DIM)
    stat = jax.ShapeDtypeStruct((pair, GROUP * rows, HEAD_DIM), F32)
    out = jax.ShapeDtypeStruct((rows, width), BF16) if last else [stat] * 3
    keys_total = sum(k.shape[0] for k in keys)
    work = pair * GROUP * rows * keys_total
    vmem = pl.BlockSpec(memory_space=pltpu.VMEM)
    return pl.pallas_call(
        functools.partial(attend_kernel, pieces, state is None, last),
        out_shape=out,
        in_specs=[vmem] * (2 + 2 * pieces + (0 if state is None else 3)),
        out_specs=vmem if last else [vmem] * 3,
        compiler_params=pltpu.CompilerParams(vmem_limit_bytes=40 << 20),
        cost_estimate=pl.CostEstimate(
            flops=4 * work * HEAD_DIM,
            bytes_accessed=4 * keys_total * pair * HEAD_DIM + 6 * 4 * stat.size,
            transcendentals=work,
        ),
    )(queries, places, *keys, *values, *(state or ()))


def in_block_ranks(ids, block_rows):
    count = ids.shape[0]
    row = jnp.arange(count, dtype=jnp.int32)
    same = ids[:, None] == ids[None, :]
    before = (row[None, :] < row[:, None]) & (
        row[None, :] // block_rows == row[:, None] // block_rows
    )
    return jnp.sum((same & before).astype(jnp.int32), axis=-1)


def ring(size, step):
    return [(i, (i + step) % size) for i in range(size)]


def per_device(
    query_rows,
    stretch_keys,
    stretch_values,
    cache_keys,
    cache_values,
    cache_len,
    residual,
    out_weight,
    norm_gain,
    router_weight,
    expert_ids,
    gate_weight,
    up_weight,
    down_weight,
):
    z = lax.axis_index("z")
    yl = lax.axis_index("yl")
    x = lax.axis_index("x")
    yh = lax.axis_index("yh")
    c = lax.axis_index("c")
    nz = lax.axis_size("z")
    nx = lax.axis_size("x")
    rows = query_rows.shape[1]
    cache_rows = cache_keys.shape[1]
    width = query_rows.shape[2]
    half = width // 2
    kv_width = cache_keys.shape[2]
    kv_half = kv_width // 2
    seqs = residual.shape[0]
    cols = residual.shape[2]
    model = cols * lax.axis_size(E_AXES)
    experts = gate_weight.shape[0] * lax.axis_size(E_AXES)

    first_half = yl
    keys_own = jnp.concatenate([cache_keys[0], stretch_keys[0]], axis=0)
    values_own = jnp.concatenate([cache_values[0], stretch_values[0]], axis=0)

    def halves(array, size):
        def pick(h):
            return lax.dynamic_slice_in_dim(array, h * size, size, 1)

        return pick(first_half), pick(1 - first_half)

    straight = [(y * 2 + k, k * 2 + y) for y in range(2) for k in range(2)]
    crossed = [(y * 2 + k, k * 2 + 1 - y) for y in range(2) for k in range(2)]

    def to_chip(array, size):
        a, b = halves(array, size)
        a = lax.ppermute(a, ("yl", "c"), straight)
        b = lax.ppermute(b, ("yl", "c"), crossed)
        return jnp.concatenate([jnp.where(c == 0, a, b), jnp.where(c == 0, b, a)], axis=0)

    with jax.named_scope("to_chip"):
        keys0 = to_chip(keys_own, kv_half)
        values0 = to_chip(values_own, kv_half)
        queries = to_chip(query_rows[0], half)
        length = lax.ppermute(
            jnp.broadcast_to(cache_len.astype(F32), (8, 128)), ("yl", "c"), straight
        )[0, 0].astype(jnp.int32)

    with jax.named_scope("residual_move"):
        moved = residual.reshape(nx, 2, 2, rows, cols).transpose(0, 2, 1, 3, 4)
        moved = moved.reshape(nx * 2, 2, rows, cols)
        moved = lax.all_to_all(moved, ("x", "yl"), 0, 0, tiled=True)
        residual_rows = moved.reshape(nx, 2, 2, rows, cols).transpose(2, 1, 3, 0, 4)
        residual_rows = residual_rows.reshape(4 * rows, nx * cols)

    with jax.named_scope("out_weight_gather"):
        weight_cols = lax.all_gather(out_weight, "x", axis=1, tiled=True)

    with jax.named_scope("weight_swap"):
        gate_out, up_out, down_out, _ = lax.optimization_barrier(
            (gate_weight, up_weight, down_weight, keys0)
        )
        swap = [(0, 1), (1, 0)]

        def give(array):
            return lax.ppermute(lax.dynamic_index_in_dim(array, 1 - yl, 0, False), "yl", swap)

        gate_got, up_got, down_got = give(gate_out), give(up_out), give(down_out)

    span = rows + cache_rows

    def places(offset):
        holder = (z + offset) % nz
        r = jnp.arange(2 * span, dtype=jnp.int32)
        block, within = r // span, r % span
        slot = (holder * 2 + block) * cache_rows + within
        stretch = ((holder - z) * 2 + block) * rows + within - cache_rows
        return jnp.where(
            within < cache_rows, jnp.where(slot < length, -FAR, FAR), stretch
        )[None, :]

    with jax.named_scope("attention"):
        up_k, up_v, down_k, down_v = keys0, values0, keys0, values0
        state = attend(queries, jnp.stack([places(0)]), [keys0], [values0], None, False)
        for step in range(1, nz // 2):
            up_k = lax.ppermute(up_k, "z", ring(nz, 1))
            down_k = lax.ppermute(down_k, "z", ring(nz, -1))
            up_v = lax.ppermute(up_v, "z", ring(nz, 1))
            down_v = lax.ppermute(down_v, "z", ring(nz, -1))
            state = attend(
                queries,
                jnp.stack([places(-step), places(step)]),
                [up_k, down_k],
                [up_v, down_v],
                state,
                False,
            )
        far_k = lax.ppermute(up_k, "z", ring(nz, 1))
        far_v = lax.ppermute(down_v, "z", ring(nz, -1))
        attended = attend(
            queries, jnp.stack([places(nz // 2)]), [far_k], [far_v], state, True
        )

    with jax.named_scope("out_projection"):
        other = lax.ppermute(attended, "yh", [(0, 1), (1, 0)])
        both = jnp.concatenate(
            [jnp.where(yh == 0, attended, other), jnp.where(yh == 0, other, attended)], axis=0
        )
        both_far = lax.ppermute(both, "c", [(0, 1), (1, 0)])
        near_w = lax.dynamic_slice_in_dim(weight_cols, c * half, half, 0)
        far_w = lax.dynamic_slice_in_dim(weight_cols, (1 - c) * half, half, 0)
        projected = jnp.dot(both, near_w, preferred_element_type=F32) + jnp.dot(
            both_far, far_w, preferred_element_type=F32
        )
        hidden = (residual_rows.astype(F32) + projected).astype(BF16)

    ids = expert_ids[..., 0].reshape(nx, 2, 2, nz, 2, rows)

    with jax.named_scope("slots"):
        here = lax.dynamic_index_in_dim(ids, z, 3, False)
        source_ids = lax.dynamic_index_in_dim(here, x, 0, False)
        source_ids = lax.dynamic_index_in_dim(source_ids, yl, 1, False).reshape(4 * rows)
        ranks = in_block_ranks(source_ids, rows)
        wanted = jnp.arange(experts * 4 * CAP, dtype=jnp.int32)
        wanted_expert = wanted // (4 * CAP)
        wanted_block = wanted // CAP % 4
        wanted_rank = wanted % CAP
        row_block = jnp.arange(4 * rows, dtype=jnp.int32) // rows
        pick = (
            (wanted_expert[:, None] == source_ids[None, :])
            & (wanted_rank[:, None] == ranks[None, :])
            & (wanted_block[:, None] == row_block[None, :])
        ).astype(BF16)
        home_ids = lax.dynamic_index_in_dim(here, yl, 3, False).reshape(seqs * rows)
        same = home_ids.reshape(seqs, rows)
        earlier = jnp.arange(rows)[None, :] < jnp.arange(rows)[:, None]
        home_ranks = jnp.sum(
            ((same[:, :, None] == same[:, None, :]) & earlier[None]).astype(jnp.int32), axis=-1
        )
        code = same * CAP + home_ranks
        put = (code[:, :, None] == jnp.arange(experts * CAP, dtype=jnp.int32)).astype(BF16)

    with jax.named_scope("dispatch"):
        outgoing = jnp.dot(pick, hidden, preferred_element_type=F32).astype(BF16)
        outgoing = outgoing.reshape(experts, 4 * CAP, nx * cols)
        arriving = lax.all_to_all(outgoing, PLANE, 0, 0, tiled=True)
        arriving = arriving.reshape(nx, 2, 2, 2, 2, 2 * CAP, nx, cols)
        arriving = arriving.transpose(0, 4, 3, 5, 6, 1, 2, 7)
        slots = seqs * 2 * CAP
        arriving = arriving.reshape(slots, model)

    with jax.named_scope("hidden_home"):
        home = hidden.reshape(2, 2, rows, nx, cols).transpose(3, 1, 0, 2, 4)
        home = home.reshape(nx * 2, 2, rows, cols)
        home = lax.all_to_all(home, ("x", "yl"), 0, 0, tiled=True)
        home = home.reshape(nx, 2, 2, rows, cols).transpose(0, 2, 1, 3, 4)
        home = home.reshape(seqs, rows, cols)

    with jax.named_scope("gate"):
        numbers = arriving.astype(F32)
        mean_square = jnp.mean(numbers * numbers, axis=-1, keepdims=True)
        normed = numbers * lax.rsqrt(mean_square + EPSILON) * norm_gain.astype(F32)
        router = lax.dynamic_index_in_dim(router_weight, yl, 1, False).astype(F32)
        logits = jnp.sum(normed * router[None, :], axis=-1, keepdims=True)
        routed = (jax.nn.sigmoid(logits) * normed).astype(BF16)

    with jax.named_scope("experts"):
        tokens = lax.all_gather(routed, "z", axis=0, tiled=True)

        def mine(array):
            return lax.dynamic_index_in_dim(array, yl, 0, False)

        def expert(gate_w, up_w, down_w):
            g = jnp.dot(tokens, gate_w, preferred_element_type=F32)
            u = jnp.dot(tokens, up_w, preferred_element_type=F32)
            a = (jax.nn.silu(g) * u).astype(BF16)
            return jnp.dot(a, down_w, preferred_element_type=F32)

        partial = expert(mine(gate_weight), mine(up_weight), mine(down_weight)) + expert(
            gate_got, up_got, down_got
        )
        reduced = lax.psum_scatter(partial.astype(BF16), "z", scatter_dimension=0, tiled=True)

    with jax.named_scope("return"):
        back = reduced.reshape(seqs, 2, CAP, experts // 2, cols).transpose(3, 1, 0, 2, 4)
        back = back.reshape(experts, seqs, CAP, cols)
        back = lax.all_to_all(back, PLANE, 0, 0, tiled=True)
        back = back.transpose(1, 0, 2, 3).reshape(seqs, experts * CAP, cols)
        expert_out = jnp.einsum("src,scd->srd", put, back, preferred_element_type=F32)
        return (home.astype(F32) + expert_out).astype(BF16)


def solution(mesh):
    fine = Mesh(mesh.devices.reshape(8, 2, 4, 2, 2), ("z", "yl", "x", "yh", "c"))
    ctx = ("z", "yl")
    in_specs = (
        P(E_AXES, ctx, None),
        P(E_AXES, ctx, None),
        P(E_AXES, ctx, None),
        P(E_AXES, ctx, None),
        P(E_AXES, ctx, None),
        P(E_AXES),
        P(None, ctx, E_AXES),
        P(None, E_AXES),
        P(),
        P(None, E_AXES),
        P(),
        P(E_AXES, None, ctx),
        P(E_AXES, None, ctx),
        P(E_AXES, ctx, None),
    )
    out_specs = P(None, ctx, E_AXES)
    return jax.shard_map(
        per_device, mesh=fine, in_specs=in_specs, out_specs=out_specs, check_vma=False
    )
```

```python
import functools
import math

import jax
import jax.numpy as jnp
from jax import lax
from jax.experimental import pallas as pl
from jax.experimental.pallas import tpu as pltpu
from jax.sharding import Mesh, PartitionSpec as P

HEADS = 20
KV_HEADS = 4
HEAD_DIM = 128
GROUP = HEADS // KV_HEADS
CAP = 3
EPSILON = 1e-05
FAR = 1 << 30
FILL = -1e30
LOW = -1e20
E_AXES = ("x", "yh", "c")
PLANE = ("x", "yh", "c", "yl")
F32 = jnp.float32
BF16 = jnp.bfloat16


def attend_kernel(pieces, first, last, *refs):
    q_ref, place_ref = refs[0], refs[1]
    key_refs = refs[2 : 2 + pieces]
    value_refs = refs[2 + pieces : 2 + 2 * pieces]
    rest = refs[2 + 2 * pieces :]
    if not first:
        m_in, l_in, a_in = rest[:3]
        rest = rest[3:]
    rows = q_ref.shape[0]
    pair = q_ref.shape[1] // (GROUP * HEAD_DIM)
    factor = math.log2(math.e) / math.sqrt(HEAD_DIM)
    own = lax.broadcasted_iota(jnp.int32, (GROUP * rows, 1), 0) % rows
    for j in range(pair):
        queries = jnp.concatenate(
            [
                q_ref[:, (j * GROUP + g) * HEAD_DIM : (j * GROUP + g + 1) * HEAD_DIM]
                for g in range(GROUP)
            ],
            axis=0,
        )
        lanes = slice(j * HEAD_DIM, (j + 1) * HEAD_DIM)
        scores = []
        for i in range(pieces):
            s = lax.dot_general(
                queries,
                key_refs[i][:, lanes],
                (((1,), (1,)), ((), ())),
                preferred_element_type=F32,
            )
            scores.append(jnp.where(place_ref[i] <= own, s * factor, FILL))
        top = functools.reduce(
            jnp.maximum, [jnp.max(s, axis=-1, keepdims=True) for s in scores]
        )
        if first:
            m_new = jnp.maximum(top, LOW)
        else:
            m_old = m_in[j]
            m_new = jnp.maximum(m_old, top)
            alpha = jnp.exp2(m_old - m_new)
        high = m_new[:, :1]
        total = 0.0
        summed = 0.0
        for i in range(pieces):
            p = jnp.exp2(scores[i] - high)
            total = total + jnp.sum(p, axis=-1, keepdims=True)
            summed = summed + jnp.dot(
                p.astype(BF16), value_refs[i][:, lanes], preferred_element_type=F32
            )
        if not first:
            total = l_in[j] * alpha + total
            summed = a_in[j] * alpha + summed
        if last:
            result = (summed / total).astype(BF16)
            for g in range(GROUP):
                rest[0][:, (j * GROUP + g) * HEAD_DIM : (j * GROUP + g + 1) * HEAD_DIM] = result[
                    g * rows : (g + 1) * rows
                ]
        else:
            shape = (GROUP * rows, HEAD_DIM)
            rest[0][j] = jnp.broadcast_to(m_new, shape)
            rest[1][j] = jnp.broadcast_to(total, shape)
            rest[2][j] = summed


def attend(queries, places, keys, values, state, last):
    pieces = len(keys)
    rows, width = queries.shape
    pair = width // (GROUP * HEAD_DIM)
    stat = jax.ShapeDtypeStruct((pair, GROUP * rows, HEAD_DIM), F32)
    out = jax.ShapeDtypeStruct((rows, width), BF16) if last else [stat] * 3
    keys_total = sum(k.shape[0] for k in keys)
    work = pair * GROUP * rows * keys_total
    vmem = pl.BlockSpec(memory_space=pltpu.VMEM)
    return pl.pallas_call(
        functools.partial(attend_kernel, pieces, state is None, last),
        out_shape=out,
        in_specs=[vmem] * (2 + 2 * pieces + (0 if state is None else 3)),
        out_specs=vmem if last else [vmem] * 3,
        compiler_params=pltpu.CompilerParams(vmem_limit_bytes=40 << 20),
        cost_estimate=pl.CostEstimate(
            flops=4 * work * HEAD_DIM,
            bytes_accessed=4 * keys_total * pair * HEAD_DIM + 6 * 4 * stat.size,
            transcendentals=work,
        ),
    )(queries, places, *keys, *values, *(state or ()))


def project_kernel(own, other, far_own, far_other, weight, residual, pick, hidden, outgoing):
    rows = own.shape[0]
    half = own.shape[1]
    c = lax.axis_index("c")
    near_w = weight[pl.ds(pl.multiple_of(c * half, half), half), :]
    far_w = weight[pl.ds(pl.multiple_of((1 - c) * half, half), half), :]
    for part, (near, far) in enumerate(((own, far_own), (other, far_other))):
        here = slice(part * rows, (part + 1) * rows)
        projected = jnp.dot(near[...], near_w, preferred_element_type=F32) + jnp.dot(
            far[...], far_w, preferred_element_type=F32
        )
        hidden[here, :] = (residual[here, :].astype(F32) + projected).astype(BF16)
    outgoing[...] = jnp.dot(pick[...], hidden[...], preferred_element_type=F32).astype(BF16)


def gate_kernel(arriving, gain, router, first, second):
    slots = first.shape[0] + second.shape[0]
    group_cols = arriving.shape[2]
    sources = arriving.shape[0] // 4
    room = arriving.shape[1]
    row = lax.broadcasted_iota(jnp.int32, (slots, sources * room), 0)
    wanted = lax.broadcasted_iota(jnp.int32, (slots, sources * room), 1)
    rank = row % CAP
    seq = row // CAP % 8 + row // (16 * CAP) * 8
    block = row // (8 * CAP) % 2
    source = (seq // 4 * 2 + seq % 2) * room + seq // 2 % 2 * 8 + block * 4 + rank
    compact = jnp.where(source == wanted, 1.0, 0.0).astype(BF16)
    groups = []
    for g in range(4):
        yh, c = g // 2, g % 2
        stacked = jnp.concatenate(
            [arriving[((x * 2 + yh) * 2 + c) * 2 + yl] for x in range(sources // 2) for yl in range(2)],
            axis=0,
        )
        groups.append(jnp.dot(compact, stacked, preferred_element_type=F32))
    numbers = jnp.concatenate(groups, axis=1)
    mean_square = jnp.mean(numbers * numbers, axis=-1, keepdims=True)
    normed = numbers * lax.rsqrt(mean_square + EPSILON) * gain[...]
    logits = jnp.sum(normed * router[...], axis=-1, keepdims=True)
    routed = (normed / (1.0 + jnp.exp(-logits))).astype(BF16)
    first[...] = routed[: slots // 2]
    second[...] = routed[slots // 2 :]


def expert_kernel(pieces, *refs):
    token_refs = refs[:pieces]
    weights = refs[pieces : pieces + 6]
    outs = refs[pieces + 6 :]
    rows = token_refs[0].shape[0]
    tokens = jnp.concatenate([t[...] for t in token_refs], axis=0)
    total = 0.0
    for w in range(2):
        gate_w, up_w, down_w = weights[3 * w : 3 * w + 3]
        g = jnp.dot(tokens, gate_w[...], preferred_element_type=F32)
        u = jnp.dot(tokens, up_w[...], preferred_element_type=F32)
        a = (g / (1.0 + jnp.exp(-g)) * u).astype(BF16)
        total = total + jnp.dot(a, down_w[...], preferred_element_type=F32)
    total = total.astype(BF16)
    for i in range(pieces):
        outs[i][...] = total[i * rows : (i + 1) * rows]


def run_experts(tokens, weights):
    pieces = len(tokens)
    rows, model = tokens[0].shape
    vmem = pl.BlockSpec(memory_space=pltpu.VMEM)
    size = sum(w.size for w in weights)
    return pl.pallas_call(
        functools.partial(expert_kernel, pieces),
        out_shape=[jax.ShapeDtypeStruct((rows, model), BF16)] * pieces,
        in_specs=[vmem] * (pieces + 6),
        out_specs=[vmem] * pieces,
        compiler_params=pltpu.CompilerParams(vmem_limit_bytes=36 << 20),
        cost_estimate=pl.CostEstimate(
            flops=2 * pieces * rows * size,
            bytes_accessed=2 * size + 4 * pieces * rows * model,
            transcendentals=pieces * rows * 512,
        ),
    )(*tokens, *weights)


def in_block_ranks(ids, block_rows):
    count = ids.shape[0]
    row = jnp.arange(count, dtype=jnp.int32)
    same = ids[:, None] == ids[None, :]
    before = (row[None, :] < row[:, None]) & (
        row[None, :] // block_rows == row[:, None] // block_rows
    )
    return jnp.sum((same & before).astype(jnp.int32), axis=-1)


def ring(size, step):
    return [(i, (i + step) % size) for i in range(size)]


def per_device(
    query_rows,
    stretch_keys,
    stretch_values,
    cache_keys,
    cache_values,
    cache_len,
    residual,
    out_weight,
    norm_gain,
    router_weight,
    expert_ids,
    gate_weight,
    up_weight,
    down_weight,
):
    z = lax.axis_index("z")
    yl = lax.axis_index("yl")
    x = lax.axis_index("x")
    yh = lax.axis_index("yh")
    c = lax.axis_index("c")
    nz = lax.axis_size("z")
    nx = lax.axis_size("x")
    rows = query_rows.shape[1]
    cache_rows = cache_keys.shape[1]
    width = query_rows.shape[2]
    half = width // 2
    kv_width = cache_keys.shape[2]
    kv_half = kv_width // 2
    seqs = residual.shape[0]
    cols = residual.shape[2]
    model = cols * lax.axis_size(E_AXES)
    experts = gate_weight.shape[0] * lax.axis_size(E_AXES)

    first_half = yl
    keys_own = jnp.concatenate([cache_keys[0], stretch_keys[0]], axis=0)
    values_own = jnp.concatenate([cache_values[0], stretch_values[0]], axis=0)

    def halves(array, size):
        def pick(h):
            return lax.dynamic_slice_in_dim(array, h * size, size, 1)

        return pick(first_half), pick(1 - first_half)

    straight = [(y * 2 + k, k * 2 + y) for y in range(2) for k in range(2)]
    crossed = [(y * 2 + k, k * 2 + 1 - y) for y in range(2) for k in range(2)]

    def to_chip(array, size):
        a, b = halves(array, size)
        a = lax.ppermute(a, ("yl", "c"), straight)
        b = lax.ppermute(b, ("yl", "c"), crossed)
        return jnp.concatenate([jnp.where(c == 0, a, b), jnp.where(c == 0, b, a)], axis=0)

    with jax.named_scope("to_chip"):
        keys0 = to_chip(keys_own, kv_half)
        values0 = to_chip(values_own, kv_half)
        queries = to_chip(query_rows[0], half)
        length = lax.ppermute(
            jnp.broadcast_to(cache_len.astype(F32), (8, 128)), ("yl", "c"), straight
        )[0, 0].astype(jnp.int32)

    with jax.named_scope("residual_move"):
        moved = residual.reshape(nx, 2, 2, rows, cols).transpose(0, 2, 1, 3, 4)
        moved = moved.reshape(nx * 2, 2, rows, cols)
        moved = lax.all_to_all(moved, ("x", "yl"), 0, 0, tiled=True)
        moved = moved.reshape(nx, 2, 2, rows, cols).transpose(2, 1, 3, 0, 4)
        moved = jnp.where(yh == 0, moved, moved[::-1])
        residual_rows = moved.reshape(4 * rows, nx * cols)

    with jax.named_scope("out_weight_gather"):
        weight_cols = lax.all_gather(out_weight, "x", axis=1, tiled=True)

    def regroup(array):
        shape = array.shape
        array = array.reshape((nx, 2, 2, cols) + shape[1:])
        array = array.transpose((1, 2, 0, 3) + tuple(range(4, array.ndim)))
        return array.reshape(shape)

    def pick_expert(array, index):
        return lax.dynamic_index_in_dim(array, index, 0, False)

    with jax.named_scope("weight_swap"):
        gate_out, up_out, down_out, _ = lax.optimization_barrier(
            (gate_weight, up_weight, down_weight, keys0)
        )
        swap = [(0, 1), (1, 0)]
        gate_got = lax.ppermute(regroup(pick_expert(gate_out, 1 - yl)), "yl", swap)
        up_got = lax.ppermute(regroup(pick_expert(up_out, 1 - yl)), "yl", swap)
        down_got = lax.ppermute(pick_expert(down_out, 1 - yl), "yl", swap)
        gate_own = regroup(pick_expert(gate_out, yl))
        up_own = regroup(pick_expert(up_out, yl))
        down_own = pick_expert(down_out, yl)

    span = rows + cache_rows

    def places(offset):
        holder = (z + offset) % nz
        r = jnp.arange(2 * span, dtype=jnp.int32)
        block, within = r // span, r % span
        slot = (holder * 2 + block) * cache_rows + within
        stretch = ((holder - z) * 2 + block) * rows + within - cache_rows
        return jnp.where(
            within < cache_rows, jnp.where(slot < length, -FAR, FAR), stretch
        )[None, :]

    with jax.named_scope("attention"):
        up_k, up_v, down_k, down_v = keys0, values0, keys0, values0
        state = attend(queries, jnp.stack([places(0)]), [keys0], [values0], None, False)
        for step in range(1, nz // 2):
            up_k = lax.ppermute(up_k, "z", ring(nz, 1))
            down_k = lax.ppermute(down_k, "z", ring(nz, -1))
            up_v = lax.ppermute(up_v, "z", ring(nz, 1))
            down_v = lax.ppermute(down_v, "z", ring(nz, -1))
            state = attend(
                queries,
                jnp.stack([places(-step), places(step)]),
                [up_k, down_k],
                [up_v, down_v],
                state,
                False,
            )
            if step == 2:
                state, gate_got, residual_rows = lax.optimization_barrier(
                    (state, gate_got, residual_rows)
                )
        far_k = lax.ppermute(up_k, "z", ring(nz, 1))
        far_v = lax.ppermute(down_v, "z", ring(nz, -1))
        far_k, gate_own, up_own, down_own = lax.optimization_barrier(
            (far_k, gate_own, up_own, down_own)
        )
        attended = attend(
            queries, jnp.stack([places(nz // 2)]), [far_k], [far_v], state, True
        )
        attended, up_got = lax.optimization_barrier((attended, up_got))

    ids = expert_ids[..., 0].reshape(nx, 2, 2, nz, 2, rows)

    with jax.named_scope("slots"):
        here = lax.dynamic_index_in_dim(ids, z, 3, False)
        source_ids = lax.dynamic_index_in_dim(here, x, 0, False)
        source_ids = lax.dynamic_index_in_dim(source_ids, yl, 1, False)
        source_ids = jnp.where(yh == 0, source_ids, source_ids[::-1]).reshape(4 * rows)
        ranks = in_block_ranks(source_ids, rows)
        wanted = jnp.arange(experts * 16, dtype=jnp.int32)
        wanted_expert = wanted // 16
        wanted_block = wanted // 4 % 4
        wanted_rank = wanted % 4
        row_block = jnp.arange(4 * rows, dtype=jnp.int32) // rows ^ (yh * 2)
        pick = (
            (wanted_expert[:, None] == source_ids[None, :])
            & (wanted_rank[:, None] == ranks[None, :])
            & (wanted_block[:, None] == row_block[None, :])
        ).astype(BF16)
        same = lax.dynamic_index_in_dim(here, yl, 3, False).reshape(seqs, rows)
        earlier = jnp.arange(rows)[None, :] < jnp.arange(rows)[:, None]
        home_ranks = jnp.sum(
            ((same[:, :, None] == same[:, None, :]) & earlier[None]).astype(jnp.int32), axis=-1
        )
        part = seqs // 2
        code = (same * part + (jnp.arange(seqs) % part)[:, None]) * CAP + home_ranks
        table = jnp.arange(experts * part * CAP, dtype=jnp.int32)
        put = (code.reshape(2, part * rows, 1) == table).astype(BF16)

    vmem = pl.BlockSpec(memory_space=pltpu.VMEM)

    with jax.named_scope("out_projection"):
        other = lax.ppermute(attended, "yh", swap)
        far_own = lax.ppermute(attended, "c", swap)
        far_other = lax.ppermute(other, "c", swap)
        hidden, outgoing = pl.pallas_call(
            project_kernel,
            out_shape=[
                jax.ShapeDtypeStruct((4 * rows, nx * cols), BF16),
                jax.ShapeDtypeStruct((experts * 16, nx * cols), BF16),
            ],
            in_specs=[vmem] * 7,
            out_specs=[vmem] * 2,
            compiler_params=pltpu.CompilerParams(vmem_limit_bytes=36 << 20),
        )(attended, other, far_own, far_other, weight_cols, residual_rows, pick)

    with jax.named_scope("dispatch"):
        outgoing, down_got, put = lax.optimization_barrier((outgoing, down_got, put))
        outgoing = outgoing.reshape(experts, 16, nx * cols)
        arriving = lax.all_to_all(outgoing, PLANE, 0, 0, tiled=True)

    with jax.named_scope("gate"):
        gain = regroup(norm_gain.astype(F32))[None, :]
        router = regroup(lax.dynamic_index_in_dim(router_weight, yl, 1, False).astype(F32))[None, :]
        slots = seqs * 2 * CAP
        routed = pl.pallas_call(
            gate_kernel,
            out_shape=[jax.ShapeDtypeStruct((slots // 2, model), BF16)] * 2,
            in_specs=[vmem] * 3,
            out_specs=[vmem] * 2,
            compiler_params=pltpu.CompilerParams(vmem_limit_bytes=36 << 20),
        )(arriving, gain, router)

    with jax.named_scope("hidden_home"):
        home = hidden.reshape(2, 2, rows, nx, cols).transpose(3, 1, 0, 2, 4)
        home = home.reshape(nx * 2, 2, rows, cols)
        home = lax.all_to_all(home, ("x", "yl"), 0, 0, tiled=True)
        home = home.reshape(nx, 2, 2, rows, cols).transpose(0, 2, 1, 3, 4)
        home = jnp.where(yh == 0, home, home[:, ::-1])
        home = home.reshape(2, part * rows, cols)

    weights = (gate_own, up_own, down_own, gate_got, up_got, down_got)

    with jax.named_scope("experts"):
        up_send, down_send = ring(nz, 1), ring(nz, -1)
        own = run_experts(list(routed), weights)
        up, down = list(routed), list(routed)
        from_below, from_above = {}, {}
        for k in range(1, nz // 2):
            up = [lax.ppermute(t, "z", up_send) for t in up]
            down = [lax.ppermute(t, "z", down_send) for t in down]
            outs = run_experts(up + down, weights)
            from_below[k], from_above[k] = outs[:2], outs[2:]
        far = [lax.ppermute(up[0], "z", up_send), lax.ppermute(down[1], "z", down_send)]
        far = run_experts(far, weights)

        def add(a, b):
            return (a.astype(F32) + b.astype(F32)).astype(BF16)

        up_sum = [lax.ppermute(far[0], "z", up_send), None]
        down_sum = [None, lax.ppermute(far[1], "z", down_send)]
        for k in range(nz // 2 - 1, 0, -1):
            for h in range(2):
                mine = from_above[k][h]
                mine = mine if up_sum[h] is None else add(mine, up_sum[h])
                up_sum[h] = lax.ppermute(mine, "z", up_send)
                mine = from_below[k][h]
                mine = mine if down_sum[h] is None else add(mine, down_sum[h])
                down_sum[h] = lax.ppermute(mine, "z", down_send)
        reduced = [
            (
                own[h].astype(F32) + up_sum[h].astype(F32) + down_sum[h].astype(F32)
            ).astype(BF16)
            for h in range(2)
        ]

    with jax.named_scope("return"):
        results = []
        for h in range(2):
            back = reduced[h].reshape(2, part * CAP, experts // 2, cols).transpose(2, 0, 1, 3)
            back = back.reshape(experts, part * CAP, cols)
            back = lax.all_to_all(back, PLANE, 0, 0, tiled=True)
            back = back.reshape(experts * part * CAP, cols)
            expert_out = jnp.dot(put[h], back, preferred_element_type=F32)
            results.append((home[h].astype(F32) + expert_out).astype(BF16))
        return jnp.stack(results).reshape(seqs, rows, cols)


def solution(mesh):
    fine = Mesh(mesh.devices.reshape(8, 2, 4, 2, 2), ("z", "yl", "x", "yh", "c"))
    ctx = ("z", "yl")
    in_specs = (
        P(E_AXES, ctx, None),
        P(E_AXES, ctx, None),
        P(E_AXES, ctx, None),
        P(E_AXES, ctx, None),
        P(E_AXES, ctx, None),
        P(E_AXES),
        P(None, ctx, E_AXES),
        P(None, E_AXES),
        P(),
        P(None, E_AXES),
        P(),
        P(E_AXES, None, ctx),
        P(E_AXES, None, ctx),
        P(E_AXES, ctx, None),
    )
    out_specs = P(None, ctx, E_AXES)
    return jax.shard_map(
        per_device, mesh=fine, in_specs=in_specs, out_specs=out_specs, check_vma=False
    )
```

```python
import functools
import math

import jax
import jax.numpy as jnp
from jax import lax
from jax.experimental import pallas as pl
from jax.experimental.pallas import tpu as pltpu
from jax.sharding import Mesh, PartitionSpec as P

HEADS = 20
KV_HEADS = 4
HEAD_DIM = 128
GROUP = HEADS // KV_HEADS
CAP = 3
EPSILON = 1e-05
FAR = 1 << 30
FILL = -1e30
LOW = -1e20
E_AXES = ("x", "yh", "c")
PLANE = ("x", "yh", "c", "yl")
F32 = jnp.float32
BF16 = jnp.bfloat16


def attend_kernel(pieces, first, last, *refs):
    q_ref, place_ref = refs[0], refs[1]
    key_refs = refs[2 : 2 + pieces]
    value_refs = refs[2 + pieces : 2 + 2 * pieces]
    rest = refs[2 + 2 * pieces :]
    if not first:
        m_in, l_in, a_in = rest[:3]
        rest = rest[3:]
    rows = q_ref.shape[0]
    pair = q_ref.shape[1] // (GROUP * HEAD_DIM)
    factor = math.log2(math.e) / math.sqrt(HEAD_DIM)
    own = lax.broadcasted_iota(jnp.int32, (GROUP * rows, 1), 0) % rows
    for j in range(pair):
        queries = jnp.concatenate(
            [
                q_ref[:, (j * GROUP + g) * HEAD_DIM : (j * GROUP + g + 1) * HEAD_DIM]
                for g in range(GROUP)
            ],
            axis=0,
        )
        lanes = slice(j * HEAD_DIM, (j + 1) * HEAD_DIM)
        scores = []
        for i in range(pieces):
            s = lax.dot_general(
                queries,
                key_refs[i][:, lanes],
                (((1,), (1,)), ((), ())),
                preferred_element_type=F32,
            )
            scores.append(jnp.where(place_ref[i] <= own, s * factor, FILL))
        top = functools.reduce(
            jnp.maximum, [jnp.max(s, axis=-1, keepdims=True) for s in scores]
        )
        if first:
            m_new = jnp.maximum(top, LOW)
        else:
            m_old = m_in[j]
            m_new = jnp.maximum(m_old, top)
            alpha = jnp.exp2(m_old - m_new)
        high = m_new[:, :1]
        total = 0.0
        summed = 0.0
        for i in range(pieces):
            p = jnp.exp2(scores[i] - high)
            total = total + jnp.sum(p, axis=-1, keepdims=True)
            summed = summed + jnp.dot(
                p.astype(BF16), value_refs[i][:, lanes], preferred_element_type=F32
            )
        if not first:
            total = l_in[j] * alpha + total
            summed = a_in[j] * alpha + summed
        if last:
            result = (summed / total).astype(BF16)
            for g in range(GROUP):
                rest[0][:, (j * GROUP + g) * HEAD_DIM : (j * GROUP + g + 1) * HEAD_DIM] = result[
                    g * rows : (g + 1) * rows
                ]
        else:
            shape = (GROUP * rows, HEAD_DIM)
            rest[0][j] = jnp.broadcast_to(m_new, shape)
            rest[1][j] = jnp.broadcast_to(total, shape)
            rest[2][j] = summed


def attend(queries, places, keys, values, state, last):
    pieces = len(keys)
    rows, width = queries.shape
    pair = width // (GROUP * HEAD_DIM)
    stat = jax.ShapeDtypeStruct((pair, GROUP * rows, HEAD_DIM), F32)
    out = jax.ShapeDtypeStruct((rows, width), BF16) if last else [stat] * 3
    keys_total = sum(k.shape[0] for k in keys)
    work = pair * GROUP * rows * keys_total
    vmem = pl.BlockSpec(memory_space=pltpu.VMEM)
    return pl.pallas_call(
        functools.partial(attend_kernel, pieces, state is None, last),
        out_shape=out,
        in_specs=[vmem] * (2 + 2 * pieces + (0 if state is None else 3)),
        out_specs=vmem if last else [vmem] * 3,
        compiler_params=pltpu.CompilerParams(vmem_limit_bytes=24 << 20),
        cost_estimate=pl.CostEstimate(
            flops=16 * 4 * work * HEAD_DIM,
            bytes_accessed=4 * keys_total * pair * HEAD_DIM + 6 * 4 * stat.size,
            transcendentals=work,
        ),
    )(queries, places, *keys, *values, *(state or ()))


def project_kernel(own, other, far_own, far_other, weight, residual, pick, token, outgoing):
    del token
    half = own.shape[1]
    c = lax.axis_index("c")
    yh = lax.axis_index("yh")
    near_w = weight[:, pl.ds(pl.multiple_of(c * half, half), half)]
    far_w = weight[:, pl.ds(pl.multiple_of((1 - c) * half, half), half)]
    near_x = jnp.concatenate([own[...], other[...]], axis=0)
    far_x = jnp.concatenate([far_own[...], far_other[...]], axis=0)
    across = (((1,), (1,)), ((), ()))
    projected = lax.dot_general(near_x, near_w, across, preferred_element_type=F32)
    projected += lax.dot_general(far_x, far_w, across, preferred_element_type=F32)
    lead = jnp.concatenate(
        [
            jnp.concatenate(
                [residual[x * 2 + block, turn].astype(F32) for turn in (yh, 1 - yh) for block in range(2)],
                axis=0,
            )
            for x in range(residual.shape[0] // 2)
        ],
        axis=1,
    )
    hidden = (lead + projected).astype(BF16)
    outgoing[...] = jnp.dot(pick[...], hidden, preferred_element_type=F32).astype(BF16)


def gate_kernel(arriving, gain, router, first, second, rows_out):
    slots = first.shape[0] + second.shape[0]
    sources = arriving.shape[0] // 4
    room = arriving.shape[1]
    row = lax.broadcasted_iota(jnp.int32, (slots, sources * room), 0)
    wanted = lax.broadcasted_iota(jnp.int32, (slots, sources * room), 1)
    rank = row % CAP
    seq = row // CAP % 8 + row // (16 * CAP) * 8
    block = row // (8 * CAP) % 2
    source = (seq // 4 * 2 + seq % 2) * room + seq // 2 % 2 * 8 + block * 4 + rank
    compact = jnp.where(source == wanted, 1.0, 0.0).astype(BF16)
    groups = []
    for g in range(4):
        yh, c = g // 2, g % 2
        stacked = jnp.concatenate(
            [arriving[((x * 2 + yh) * 2 + c) * 2 + yl] for x in range(sources // 2) for yl in range(2)],
            axis=0,
        )
        groups.append(jnp.dot(compact, stacked, preferred_element_type=F32))
    cols = rows_out.shape[2]
    pieces = [
        groups[piece % 4][:, piece // 4 * cols : (piece // 4 + 1) * cols]
        for piece in range(rows_out.shape[0])
    ]
    numbers = jnp.concatenate(pieces, axis=1)
    step = slots // 4
    for i, piece in enumerate(pieces):
        rows_out[i] = jnp.concatenate(
            [piece[q * step : (q + 1) * step] for q in (0, 2, 1, 3)], axis=0
        ).astype(BF16)
    mean_square = jnp.mean(numbers * numbers, axis=-1, keepdims=True)
    normed = numbers * lax.rsqrt(mean_square + EPSILON) * gain[...]
    logits = jnp.sum(normed * router[...], axis=-1, keepdims=True)
    routed = (normed / (1.0 + jnp.exp(-logits))).astype(BF16)
    first[...] = routed[: slots // 2]
    second[...] = routed[slots // 2 :]


def finish_kernel(own_a, own_b, up_a, up_b, down_a, down_b, lead, out):
    halves = []
    for own, up, down in ((own_a, up_a, down_a), (own_b, up_b, down_b)):
        total = own[...].astype(F32) + up[...].astype(F32) + down[...].astype(F32)
        halves.append(total.astype(BF16).astype(F32))
    step = halves[0].shape[0] // 2
    cols = out.shape[2]
    for block in range(2):
        rows = jnp.concatenate([h[block * step : (block + 1) * step] for h in halves], axis=0)
        for piece in range(out.shape[0] // 2):
            add = lead[piece * 2 + block].astype(F32)
            out[piece * 2 + block] = (
                rows[:, piece * cols : (piece + 1) * cols] + add
            ).astype(BF16)


def expert_kernel(pieces, *refs):
    token_refs = refs[:pieces]
    weights = refs[pieces : pieces + 6]
    outs = refs[pieces + 6 :]
    rows = token_refs[0].shape[0]
    tokens = jnp.concatenate([t[...] for t in token_refs], axis=0)
    total = 0.0
    for w in range(2):
        gate_w, up_w, down_w = weights[3 * w : 3 * w + 3]
        g = jnp.dot(tokens, gate_w[...], preferred_element_type=F32)
        u = jnp.dot(tokens, up_w[...], preferred_element_type=F32)
        a = (g / (1.0 + jnp.exp(-g)) * u).astype(BF16)
        total = total + jnp.dot(a, down_w[...], preferred_element_type=F32)
    total = total.astype(BF16)
    for i in range(pieces):
        outs[i][...] = total[i * rows : (i + 1) * rows]


def run_experts(tokens, weights):
    pieces = len(tokens)
    rows, model = tokens[0].shape
    vmem = pl.BlockSpec(memory_space=pltpu.VMEM)
    size = sum(w.size for w in weights)
    return pl.pallas_call(
        functools.partial(expert_kernel, pieces),
        out_shape=[jax.ShapeDtypeStruct((rows, model), BF16)] * pieces,
        in_specs=[vmem] * (pieces + 6),
        out_specs=[vmem] * pieces,
        compiler_params=pltpu.CompilerParams(vmem_limit_bytes=24 << 20),
        cost_estimate=pl.CostEstimate(
            flops=5 * 2 * pieces * rows * size,
            bytes_accessed=2 * size + 4 * pieces * rows * model,
            transcendentals=pieces * rows * 512,
        ),
    )(*tokens, *weights)


def in_block_ranks(ids, block_rows):
    count = ids.shape[0]
    row = jnp.arange(count, dtype=jnp.int32)
    same = ids[:, None] == ids[None, :]
    before = (row[None, :] < row[:, None]) & (
        row[None, :] // block_rows == row[:, None] // block_rows
    )
    return jnp.sum((same & before).astype(jnp.int32), axis=-1)


def after(small, *arrays):
    for array in arrays:
        corner = lax.slice(array, (0,) * array.ndim, (1,) * array.ndim).reshape(())
        small, corner = lax.optimization_barrier((small, corner))
        small = jnp.maximum(small, jnp.where(corner != corner, small, small - 1))
    return small


def ring(size, step):
    return [(i, (i + step) % size) for i in range(size)]


def per_device(
    query_rows,
    stretch_keys,
    stretch_values,
    cache_keys,
    cache_values,
    cache_len,
    residual,
    out_weight,
    norm_gain,
    router_weight,
    expert_ids,
    gate_weight,
    up_weight,
    down_weight,
):
    z = lax.axis_index("z")
    yl = lax.axis_index("yl")
    x = lax.axis_index("x")
    yh = lax.axis_index("yh")
    c = lax.axis_index("c")
    nz = lax.axis_size("z")
    nx = lax.axis_size("x")
    rows = query_rows.shape[1]
    cache_rows = cache_keys.shape[1]
    width = query_rows.shape[2]
    half = width // 2
    kv_width = cache_keys.shape[2]
    kv_half = kv_width // 2
    seqs = residual.shape[0]
    cols = residual.shape[2]
    model = cols * lax.axis_size(E_AXES)
    experts = gate_weight.shape[0] * lax.axis_size(E_AXES)

    first_half = yl
    keys_own = jnp.concatenate([cache_keys[0], stretch_keys[0]], axis=0)
    values_own = jnp.concatenate([cache_values[0], stretch_values[0]], axis=0)

    def halves(array, size):
        def pick(h):
            return lax.dynamic_slice_in_dim(array, h * size, size, 1)

        return pick(first_half), pick(1 - first_half)

    straight = [(y * 2 + k, k * 2 + y) for y in range(2) for k in range(2)]
    crossed = [(y * 2 + k, k * 2 + 1 - y) for y in range(2) for k in range(2)]

    def send(array, size):
        a, b = halves(array, size)
        return lax.ppermute(a, ("yl", "c"), straight), lax.ppermute(b, ("yl", "c"), crossed)

    def join(a, b):
        return jnp.concatenate([jnp.where(c == 0, a, b), jnp.where(c == 0, b, a)], axis=0)

    with jax.named_scope("to_chip"):
        key_parts = send(keys_own, kv_half)
        value_parts = send(values_own, kv_half)
        query_parts = send(query_rows[0], half)
        keys0 = join(*key_parts)
        values0 = join(*value_parts)
        queries = join(*query_parts)
        length = lax.ppermute(
            jnp.broadcast_to(cache_len.astype(F32), (8, 128)), ("yl", "c"), straight
        )[0, 0].astype(jnp.int32)

    with jax.named_scope("out_weight_gather"):
        weight_cols = lax.all_gather(out_weight.T, "x", axis=0, tiled=True)

    def pick_expert(array, index):
        return lax.dynamic_index_in_dim(array, index, 0, False)

    with jax.named_scope("weight_swap"):
        swap = [(0, 1), (1, 0)]
        given = after(1 - yl, *query_parts)
        gate_got = lax.ppermute(pick_expert(gate_weight, given), "yl", swap)
        up_got = lax.ppermute(pick_expert(up_weight, given), "yl", swap)

    ids = expert_ids[..., 0].reshape(nx, 2, 2, nz, 2, rows)

    with jax.named_scope("slots"):
        here = lax.dynamic_index_in_dim(ids, z, 3, False)
        source_ids = lax.dynamic_index_in_dim(here, x, 0, False)
        source_ids = lax.dynamic_index_in_dim(source_ids, yl, 1, False)
        source_ids = jnp.where(yh == 0, source_ids, source_ids[::-1]).reshape(4 * rows)
        ranks = in_block_ranks(source_ids, rows)
        wanted = jnp.arange(experts * 16, dtype=jnp.int32)
        wanted_expert = wanted // 16
        wanted_block = wanted // 4 % 4
        wanted_rank = wanted % 4
        row_block = jnp.arange(4 * rows, dtype=jnp.int32) // rows ^ (yh * 2)
        pick = (
            (wanted_expert[:, None] == source_ids[None, :])
            & (wanted_rank[:, None] == ranks[None, :])
            & (wanted_block[:, None] == row_block[None, :])
        ).astype(BF16)
        same = lax.dynamic_index_in_dim(here, yl, 3, False).reshape(seqs, rows)
        earlier = jnp.arange(rows)[None, :] < jnp.arange(rows)[:, None]
        home_ranks = jnp.sum(
            ((same[:, :, None] == same[:, None, :]) & earlier[None]).astype(jnp.int32), axis=-1
        )
        code = (same * seqs + jnp.arange(seqs)[:, None]) * CAP + home_ranks
        table = jnp.arange(experts * seqs * CAP, dtype=jnp.int32)
        put = (code.reshape(seqs * rows, 1) == table).astype(BF16)

    span = rows + cache_rows

    def places(offset):
        holder = (z + offset) % nz
        r = jnp.arange(2 * span, dtype=jnp.int32)
        block, within = r // span, r % span
        slot = (holder * 2 + block) * cache_rows + within
        stretch = ((holder - z) * 2 + block) * rows + within - cache_rows
        return jnp.where(
            within < cache_rows, jnp.where(slot < length, -FAR, FAR), stretch
        )[None, :]

    with jax.named_scope("attention"):
        up_k, up_v, down_k, down_v = keys0, values0, keys0, values0
        state = attend(queries, jnp.stack([places(0)]), [keys0], [values0], None, False)
        for step in range(1, nz // 2):
            if step > 1:
                state = attend(queries, step_places, [up_k, down_k], [up_v, down_v], state, False)
            up_k = lax.ppermute(up_k, "z", ring(nz, 1))
            down_k = lax.ppermute(down_k, "z", ring(nz, -1))
            up_v = lax.ppermute(up_v, "z", ring(nz, 1))
            down_v = lax.ppermute(down_v, "z", ring(nz, -1))
            step_places = jnp.stack([places(-step), places(step)])
        far_k = lax.ppermute(up_k, "z", ring(nz, 1))
        far_v = lax.ppermute(down_v, "z", ring(nz, -1))
        state = attend(queries, step_places, [up_k, down_k], [up_v, down_v], state, False)
        attended = attend(
            queries,
            jnp.stack([after(places(nz // 2), gate_got)]),
            [far_k],
            [far_v],
            state,
            True,
        )

    vmem = pl.BlockSpec(memory_space=pltpu.VMEM)

    with jax.named_scope("out_projection"):
        other = lax.ppermute(attended, "yh", swap)
        far_own = lax.ppermute(attended, "c", swap)
        far_other = lax.ppermute(other, "c", swap)
        moved = residual.reshape(nx, 2, 2, rows, cols).transpose(0, 2, 1, 3, 4)
        moved = moved.reshape(nx * 2, 2, rows, cols)
        residual_rows = lax.all_to_all(moved, ("x", "yl"), 0, 0, tiled=True)
        outgoing = pl.pallas_call(
            project_kernel,
            out_shape=jax.ShapeDtypeStruct((experts * 16, nx * cols), BF16),
            in_specs=[vmem] * 8,
            out_specs=vmem,
            compiler_params=pltpu.CompilerParams(vmem_limit_bytes=24 << 20),
        )(
            attended,
            other,
            far_own,
            far_other,
            weight_cols,
            residual_rows,
            pick,
            up_got[:16, :128],
        )

    with jax.named_scope("dispatch"):
        outgoing = outgoing.reshape(experts, 16, nx * cols)
        arriving = lax.all_to_all(outgoing, PLANE, 0, 0, tiled=True)

    with jax.named_scope("gate"):
        gain = norm_gain.astype(F32)[None, :]
        router = lax.dynamic_index_in_dim(router_weight, yl, 1, False).astype(F32)[None, :]
        slots = seqs * 2 * CAP
        *routed, hidden = pl.pallas_call(
            gate_kernel,
            out_shape=[jax.ShapeDtypeStruct((slots // 2, model), BF16)] * 2
            + [jax.ShapeDtypeStruct((experts // 2, slots, cols), BF16)],
            in_specs=[vmem] * 3,
            out_specs=[vmem] * 3,
            compiler_params=pltpu.CompilerParams(vmem_limit_bytes=24 << 20),
        )(arriving, gain, router)

    with jax.named_scope("weight_swap"):
        down_got = lax.ppermute(pick_expert(down_weight, after(1 - yl, arriving)), "yl", swap)
        gate_own, up_own, down_own = (
            pick_expert(w, yl) for w in (gate_weight, up_weight, down_weight)
        )
    weights = (gate_own, up_own, down_own, gate_got, up_got, down_got)

    with jax.named_scope("experts"):
        up_send, down_send = ring(nz, 1), ring(nz, -1)
        up, down = [list(routed)], [list(routed)]
        for k in range(1, nz // 2):
            up.append([lax.ppermute(t, "z", up_send) for t in up[-1]])
            down.append([lax.ppermute(t, "z", down_send) for t in down[-1]])
        from_below, from_above = {}, {}
        outs = list(run_experts([*routed, *up[1], *down[1]], weights))
        own, from_below[1], from_above[1] = outs[:2], outs[2:4], outs[4:]
        far = [
            lax.ppermute(up[-1][0], "z", up_send),
            lax.ppermute(down[-1][1], "z", down_send),
        ]
        for k in range(2, nz // 2):
            outs = run_experts(up[k] + down[k], weights)
            from_below[k], from_above[k] = outs[:2], outs[2:]
        far = run_experts(far, weights)

        def add(a, b):
            return (a.astype(F32) + b.astype(F32)).astype(BF16)

        up_sum = [lax.ppermute(far[0], "z", up_send), None]
        down_sum = [None, lax.ppermute(far[1], "z", down_send)]
        for k in range(nz // 2 - 1, 0, -1):
            for h in range(2):
                mine = from_above[k][h]
                mine = mine if up_sum[h] is None else add(mine, up_sum[h])
                up_sum[h] = lax.ppermute(mine, "z", up_send)
                mine = from_below[k][h]
                mine = mine if down_sum[h] is None else add(mine, down_sum[h])
                down_sum[h] = lax.ppermute(mine, "z", down_send)

    with jax.named_scope("return"):
        lead = hidden.reshape(experts, slots // 2, cols)
        back = pl.pallas_call(
            finish_kernel,
            out_shape=jax.ShapeDtypeStruct((experts, slots // 2, cols), BF16),
            in_specs=[vmem] * 7,
            out_specs=vmem,
            compiler_params=pltpu.CompilerParams(vmem_limit_bytes=24 << 20),
        )(*own, *up_sum, *down_sum, lead)
        back = lax.all_to_all(back, PLANE, 0, 0, tiled=True)
        back = back.reshape(-1, cols)
        return jnp.dot(put, back, preferred_element_type=F32).astype(BF16).reshape(seqs, rows, cols)


def solution(mesh):
    fine = Mesh(mesh.devices.reshape(8, 2, 4, 2, 2), ("z", "yl", "x", "yh", "c"))
    ctx = ("z", "yl")
    in_specs = (
        P(E_AXES, ctx, None),
        P(E_AXES, ctx, None),
        P(E_AXES, ctx, None),
        P(E_AXES, ctx, None),
        P(E_AXES, ctx, None),
        P(E_AXES),
        P(None, ctx, E_AXES),
        P(None, E_AXES),
        P(),
        P(None, E_AXES),
        P(),
        P(E_AXES, None, ctx),
        P(E_AXES, None, ctx),
        P(E_AXES, ctx, None),
    )
    out_specs = P(None, ctx, E_AXES)
    return jax.shard_map(
        per_device, mesh=fine, in_specs=in_specs, out_specs=out_specs, check_vma=False
    )
```

```python
import functools
import math

import jax
import jax.numpy as jnp
from jax import lax
from jax.experimental import pallas as pl
from jax.experimental.pallas import tpu as pltpu
from jax.sharding import Mesh, PartitionSpec as P

HEADS = 20
KV_HEADS = 4
HEAD_DIM = 128
GROUP = HEADS // KV_HEADS
CAP = 3
EPSILON = 1e-05
FAR = 1 << 30
FILL = -1e30
LOW = -1e20
E_AXES = ("x", "yh", "c")
PLANE = ("x", "yh", "c", "yl")
F32 = jnp.float32
BF16 = jnp.bfloat16


def attend_kernel(pieces, first, last, *refs):
    q_ref, place_ref = refs[0], refs[1]
    key_refs = refs[2 : 2 + pieces]
    value_refs = refs[2 + pieces : 2 + 2 * pieces]
    rest = refs[2 + 2 * pieces :]
    if not first:
        held = rest[0]
        rest = rest[1:]
    rows = q_ref.shape[0]
    pair = q_ref.shape[1] // (GROUP * HEAD_DIM)
    factor = math.log2(math.e) / math.sqrt(HEAD_DIM)
    own = lax.broadcasted_iota(jnp.int32, (GROUP * rows, 1), 0) % rows
    for j in range(pair):
        queries = jnp.concatenate(
            [
                q_ref[:, (j * GROUP + g) * HEAD_DIM : (j * GROUP + g + 1) * HEAD_DIM]
                for g in range(GROUP)
            ],
            axis=0,
        )
        lanes = slice(j * HEAD_DIM, (j + 1) * HEAD_DIM)
        scores = []
        for i in range(pieces):
            s = lax.dot_general(
                queries,
                key_refs[i][:, lanes],
                (((1,), (1,)), ((), ())),
                preferred_element_type=F32,
            )
            scores.append(jnp.where(place_ref[i] <= own, s * factor, FILL))
        top = functools.reduce(
            jnp.maximum, [jnp.max(s, axis=-1, keepdims=True) for s in scores]
        )
        if first:
            high = jnp.maximum(top, LOW)
        else:
            m_old = held[j, :, HEAD_DIM : HEAD_DIM + 1]
            high = jnp.maximum(m_old, top)
            alpha = jnp.exp2(m_old - high)
        total = 0.0
        summed = 0.0
        for i in range(pieces):
            p = jnp.exp2(scores[i] - high)
            total = total + jnp.sum(p, axis=-1, keepdims=True)
            summed = summed + jnp.dot(
                p.astype(BF16), value_refs[i][:, lanes], preferred_element_type=F32
            )
        if not first:
            total = held[j, :, 3 * HEAD_DIM // 2 : 3 * HEAD_DIM // 2 + 1] * alpha + total
            summed = held[j, :, :HEAD_DIM] * alpha + summed
        if last:
            result = (summed / total).astype(BF16)
            for g in range(GROUP):
                rest[0][:, (j * GROUP + g) * HEAD_DIM : (j * GROUP + g + 1) * HEAD_DIM] = result[
                    g * rows : (g + 1) * rows
                ]
        else:
            lane = lax.broadcasted_iota(jnp.int32, (GROUP * rows, HEAD_DIM), 1)
            rest[0][j, :, :HEAD_DIM] = summed
            rest[0][j, :, HEAD_DIM:] = jnp.where(lane < HEAD_DIM // 2, high, total)


def attend(queries, places, keys, values, state, last):
    pieces = len(keys)
    rows, width = queries.shape
    pair = width // (GROUP * HEAD_DIM)
    stat = jax.ShapeDtypeStruct((pair, GROUP * rows, 2 * HEAD_DIM), F32)
    out = jax.ShapeDtypeStruct((rows, width), BF16) if last else stat
    keys_total = sum(k.shape[0] for k in keys)
    work = pair * GROUP * rows * keys_total
    vmem = pl.BlockSpec(memory_space=pltpu.VMEM)
    return pl.pallas_call(
        functools.partial(attend_kernel, pieces, state is None, last),
        out_shape=out,
        in_specs=[vmem] * (2 + 2 * pieces + (0 if state is None else 1)),
        out_specs=vmem,
        compiler_params=pltpu.CompilerParams(vmem_limit_bytes=24 << 20),
        cost_estimate=pl.CostEstimate(
            flops=16 * 4 * work * HEAD_DIM,
            bytes_accessed=4 * keys_total * pair * HEAD_DIM + 2 * 4 * stat.size,
            transcendentals=work,
        ),
    )(queries, places, *keys, *values, *(() if state is None else (state,)))


def project_kernel(own, other, far_own, far_other, weight, residual, pick, token, outgoing):
    del token
    half = own.shape[1]
    c = lax.axis_index("c")
    yh = lax.axis_index("yh")
    near_w = weight[:, pl.ds(pl.multiple_of(c * half, half), half)]
    far_w = weight[:, pl.ds(pl.multiple_of((1 - c) * half, half), half)]
    near_x = jnp.concatenate([own[...], other[...]], axis=0)
    far_x = jnp.concatenate([far_own[...], far_other[...]], axis=0)
    across = (((1,), (1,)), ((), ()))
    projected = lax.dot_general(near_x, near_w, across, preferred_element_type=F32)
    projected += lax.dot_general(far_x, far_w, across, preferred_element_type=F32)
    lead = jnp.concatenate(
        [
            jnp.concatenate(
                [residual[x * 2 + block, turn].astype(F32) for turn in (yh, 1 - yh) for block in range(2)],
                axis=0,
            )
            for x in range(residual.shape[0] // 2)
        ],
        axis=1,
    )
    hidden = (lead + projected).astype(BF16)
    outgoing[...] = jnp.dot(pick[...], hidden, preferred_element_type=F32).astype(BF16)


def gate_kernel(arriving, gain, router, first, second, rows_out):
    slots = first.shape[0] + second.shape[0]
    sources = arriving.shape[0] // 4
    room = arriving.shape[1]
    row = lax.broadcasted_iota(jnp.int32, (slots, sources * room), 0)
    wanted = lax.broadcasted_iota(jnp.int32, (slots, sources * room), 1)
    rank = row % CAP
    seq = row // CAP % 8 + row // (16 * CAP) * 8
    block = row // (8 * CAP) % 2
    source = (seq // 4 * 2 + seq % 2) * room + seq // 2 % 2 * 8 + block * 4 + rank
    compact = jnp.where(source == wanted, 1.0, 0.0).astype(BF16)
    groups = []
    for g in range(4):
        yh, c = g // 2, g % 2
        stacked = jnp.concatenate(
            [arriving[((x * 2 + yh) * 2 + c) * 2 + yl] for x in range(sources // 2) for yl in range(2)],
            axis=0,
        )
        groups.append(jnp.dot(compact, stacked, preferred_element_type=F32))
    cols = rows_out.shape[2]
    pieces = [
        groups[piece % 4][:, piece // 4 * cols : (piece // 4 + 1) * cols]
        for piece in range(rows_out.shape[0])
    ]
    numbers = jnp.concatenate(pieces, axis=1)
    step = slots // 4
    for i, piece in enumerate(pieces):
        rows_out[i] = jnp.concatenate(
            [piece[q * step : (q + 1) * step] for q in (0, 2, 1, 3)], axis=0
        ).astype(BF16)
    mean_square = jnp.mean(numbers * numbers, axis=-1, keepdims=True)
    normed = numbers * lax.rsqrt(mean_square + EPSILON) * gain[...]
    logits = jnp.sum(normed * router[...], axis=-1, keepdims=True)
    routed = (normed / (1.0 + jnp.exp(-logits))).astype(BF16)
    first[...] = routed[: slots // 2]
    second[...] = routed[slots // 2 :]


def finish_kernel(own_a, own_b, up_a, up_b, down_a, down_b, lead, out):
    halves = []
    for own, up, down in ((own_a, up_a, down_a), (own_b, up_b, down_b)):
        total = own[...].astype(F32) + up[...].astype(F32) + down[...].astype(F32)
        halves.append(total.astype(BF16).astype(F32))
    step = halves[0].shape[0] // 2
    cols = out.shape[2]
    for block in range(2):
        rows = jnp.concatenate([h[block * step : (block + 1) * step] for h in halves], axis=0)
        for piece in range(out.shape[0] // 2):
            add = lead[piece * 2 + block].astype(F32)
            out[piece * 2 + block] = (
                rows[:, piece * cols : (piece + 1) * cols] + add
            ).astype(BF16)


def add_kernel(a, b, c, d, first, second):
    first[...] = (a[...].astype(F32) + b[...].astype(F32)).astype(BF16)
    second[...] = (c[...].astype(F32) + d[...].astype(F32)).astype(BF16)


def add_pair(a, b, c, d):
    vmem = pl.BlockSpec(memory_space=pltpu.VMEM)
    return pl.pallas_call(
        add_kernel,
        out_shape=[jax.ShapeDtypeStruct(a.shape, BF16)] * 2,
        in_specs=[vmem] * 4,
        out_specs=[vmem] * 2,
        compiler_params=pltpu.CompilerParams(vmem_limit_bytes=8 << 20),
        cost_estimate=pl.CostEstimate(
            flops=2 * a.size, bytes_accessed=12 * a.size, transcendentals=0
        ),
    )(a, b, c, d)


def expert_kernel(pieces, *refs):
    token_refs = refs[:pieces]
    gate_own, up_own, down_own, first_got, rest_got, down_got = refs[pieces : pieces + 6]
    outs = refs[pieces + 6 :]
    model = gate_own.shape[0]
    upper = first_got.shape[0] - model
    sides = (
        (gate_own, ((up_own, 0, model),), down_own),
        (
            first_got.at[pl.ds(0, model)],
            ((first_got.at[pl.ds(model, upper)], 0, upper), (rest_got, upper, model)),
            down_got,
        ),
    )
    rows = token_refs[0].shape[0]
    for at in range(0, pieces, 8):
        tokens = jnp.concatenate([t[...] for t in token_refs[at : at + 8]], axis=0)
        total = 0.0
        for gate_w, up_parts, down_w in sides:
            g = jnp.dot(tokens, gate_w[...], preferred_element_type=F32)
            u = sum(
                jnp.dot(tokens[:, lo:hi], part[...], preferred_element_type=F32)
                for part, lo, hi in up_parts
            )
            a = (g / (1.0 + jnp.exp(-g)) * u).astype(BF16)
            total = total + jnp.dot(a, down_w[...], preferred_element_type=F32)
        total = total.astype(BF16)
        for i, out in enumerate(outs[at : at + 8]):
            out[...] = total[i * rows : (i + 1) * rows]


def run_experts(tokens, weights):
    pieces = len(tokens)
    rows, model = tokens[0].shape
    vmem = pl.BlockSpec(memory_space=pltpu.VMEM)
    size = sum(w.size for w in weights)
    return pl.pallas_call(
        functools.partial(expert_kernel, pieces),
        out_shape=[jax.ShapeDtypeStruct((rows, model), BF16)] * pieces,
        in_specs=[vmem] * (pieces + 6),
        out_specs=[vmem] * pieces,
        compiler_params=pltpu.CompilerParams(vmem_limit_bytes=36 << 20),
        cost_estimate=pl.CostEstimate(
            flops=5 * 2 * pieces * rows * size,
            bytes_accessed=2 * size + 4 * pieces * rows * model,
            transcendentals=pieces * rows * 512,
        ),
    )(*tokens, *weights)


def in_block_ranks(ids, block_rows):
    count = ids.shape[0]
    row = jnp.arange(count, dtype=jnp.int32)
    same = ids[:, None] == ids[None, :]
    before = (row[None, :] < row[:, None]) & (
        row[None, :] // block_rows == row[:, None] // block_rows
    )
    return jnp.sum((same & before).astype(jnp.int32), axis=-1)


def after(small, *arrays):
    for array in arrays:
        corner = lax.slice(array, (0,) * array.ndim, (1,) * array.ndim).reshape(())
        small, corner = lax.optimization_barrier((small, corner))
        small = jnp.maximum(small, jnp.where(corner != corner, small, small - 1))
    return small


def ring(size, step):
    return [(i, (i + step) % size) for i in range(size)]


def per_device(
    query_rows,
    stretch_keys,
    stretch_values,
    cache_keys,
    cache_values,
    cache_len,
    residual,
    out_weight,
    norm_gain,
    router_weight,
    expert_ids,
    gate_weight,
    up_weight,
    down_weight,
):
    z = lax.axis_index("z")
    yl = lax.axis_index("yl")
    x = lax.axis_index("x")
    yh = lax.axis_index("yh")
    c = lax.axis_index("c")
    nz = lax.axis_size("z")
    nx = lax.axis_size("x")
    rows = query_rows.shape[1]
    cache_rows = cache_keys.shape[1]
    width = query_rows.shape[2]
    half = width // 2
    kv_width = cache_keys.shape[2]
    kv_half = kv_width // 2
    seqs = residual.shape[0]
    cols = residual.shape[2]
    model = cols * lax.axis_size(E_AXES)
    experts = gate_weight.shape[0] * lax.axis_size(E_AXES)

    first_half = yl
    keys_own = jnp.concatenate([cache_keys[0], stretch_keys[0]], axis=0)
    values_own = jnp.concatenate([cache_values[0], stretch_values[0]], axis=0)

    def lanes(array, h, size):
        return lax.dynamic_slice_in_dim(array, h * size, size, 1)

    def keys_and_values(h):
        return jnp.concatenate(
            [lanes(keys_own, h, kv_half), lanes(values_own, h, kv_half)], axis=1
        )

    straight = [(y * 2 + k, k * 2 + y) for y in range(2) for k in range(2)]
    crossed = [(y * 2 + k, k * 2 + 1 - y) for y in range(2) for k in range(2)]

    def send(part):
        a = lax.ppermute(part(first_half), ("yl", "c"), straight)
        b = lax.ppermute(part(1 - first_half), ("yl", "c"), crossed)
        return a, b

    def join(a, b):
        return jnp.concatenate([jnp.where(c == 0, a, b), jnp.where(c == 0, b, a)], axis=0)

    with jax.named_scope("to_chip"):
        kv_parts = send(keys_and_values)
        query_parts = send(lambda h: lanes(query_rows[0], after(h, kv_parts[0]), half))
        held, residual = lax.optimization_barrier((query_parts[0], residual))
        query_parts = (held, query_parts[1])
        keys0 = join(*(p[:, :kv_half] for p in kv_parts))
        values0 = join(*(p[:, kv_half:] for p in kv_parts))
        queries = join(*query_parts)
        length = lax.ppermute(
            jnp.broadcast_to(cache_len.astype(F32), (8, 128)), ("yl", "c"), straight
        )[0, 0].astype(jnp.int32)

    with jax.named_scope("out_weight_gather"):
        weight_cols = lax.all_gather(out_weight.T, "x", axis=0, tiled=True)

    def pick_expert(array, index):
        return lax.dynamic_index_in_dim(array, index, 0, False)

    with jax.named_scope("weight_swap"):
        swap = [(0, 1), (1, 0)]
        given = after(1 - yl, *query_parts)
        upper = model // 2
        first_got = lax.ppermute(
            jnp.concatenate(
                [pick_expert(gate_weight, given), pick_expert(up_weight[:, :upper], given)], axis=0
            ),
            "yl",
            swap,
        )

    ids = expert_ids[..., 0].reshape(nx, 2, 2, nz, 2, rows)

    with jax.named_scope("slots"):
        here = lax.dynamic_index_in_dim(ids, z, 3, False)
        source_ids = lax.dynamic_index_in_dim(here, x, 0, False)
        source_ids = lax.dynamic_index_in_dim(source_ids, yl, 1, False)
        source_ids = jnp.where(yh == 0, source_ids, source_ids[::-1]).reshape(4 * rows)
        ranks = in_block_ranks(source_ids, rows)
        wanted = jnp.arange(experts * 16, dtype=jnp.int32)
        wanted_expert = wanted // 16
        wanted_block = wanted // 4 % 4
        wanted_rank = wanted % 4
        row_block = jnp.arange(4 * rows, dtype=jnp.int32) // rows ^ (yh * 2)
        pick = (
            (wanted_expert[:, None] == source_ids[None, :])
            & (wanted_rank[:, None] == ranks[None, :])
            & (wanted_block[:, None] == row_block[None, :])
        ).astype(BF16)
        same = lax.dynamic_index_in_dim(here, yl, 3, False).reshape(seqs, rows)
        earlier = jnp.arange(rows)[None, :] < jnp.arange(rows)[:, None]
        home_ranks = jnp.sum(
            ((same[:, :, None] == same[:, None, :]) & earlier[None]).astype(jnp.int32), axis=-1
        )
        code = (same * seqs + jnp.arange(seqs)[:, None]) * CAP + home_ranks
        table = jnp.arange(experts * seqs * CAP, dtype=jnp.int32)
        put = (code.reshape(seqs * rows, 1) == table).astype(BF16)

    span = rows + cache_rows

    def places(offset):
        holder = (z + offset) % nz
        r = jnp.arange(2 * span, dtype=jnp.int32)
        block, within = r // span, r % span
        slot = (holder * 2 + block) * cache_rows + within
        stretch = ((holder - z) * 2 + block) * rows + within - cache_rows
        return jnp.where(
            within < cache_rows, jnp.where(slot < length, -FAR, FAR), stretch
        )[None, :]

    with jax.named_scope("attention"):
        up_k, up_v, down_k, down_v = keys0, values0, keys0, values0
        state = None
        for step in range(1, nz // 2):
            up_k = lax.ppermute(up_k, "z", ring(nz, 1))
            down_k = lax.ppermute(down_k, "z", ring(nz, -1))
            up_v = lax.ppermute(up_v, "z", ring(nz, 1))
            down_v = lax.ppermute(down_v, "z", ring(nz, -1))
            step_keys, step_values = [up_k, down_k], [up_v, down_v]
            step_places = [places(-step), places(step)]
            if step == 1:
                step_keys.append(keys0)
                step_values.append(values0)
                step_places.append(places(0))
            state = attend(
                queries, jnp.stack(step_places), step_keys, step_values, state, False
            )
        far_k = lax.ppermute(up_k, "z", ring(nz, 1))
        far_v = lax.ppermute(down_v, "z", ring(nz, -1))
        attended = attend(
            queries,
            jnp.stack([places(nz // 2)]),
            [far_k],
            [far_v],
            state,
            True,
        )

    vmem = pl.BlockSpec(memory_space=pltpu.VMEM)

    with jax.named_scope("out_projection"):
        other = lax.ppermute(attended, "yh", swap)
        far_own = lax.ppermute(attended, "c", swap)
        far_other = lax.ppermute(other, "c", swap)
        moved = residual.reshape(nx, 2, 2, rows, cols).transpose(0, 2, 1, 3, 4)
        moved = moved.reshape(nx * 2, 2, rows, cols)
        residual_rows = lax.all_to_all(moved, ("x", "yl"), 0, 0, tiled=True)
        outgoing = pl.pallas_call(
            project_kernel,
            out_shape=jax.ShapeDtypeStruct((experts * 16, nx * cols), BF16),
            in_specs=[vmem] * 8,
            out_specs=vmem,
            compiler_params=pltpu.CompilerParams(vmem_limit_bytes=24 << 20),
        )(
            attended,
            other,
            far_own,
            far_other,
            weight_cols,
            residual_rows,
            pick,
            first_got[:16, :128],
        )

    with jax.named_scope("dispatch"):
        outgoing = outgoing.reshape(experts, 16, nx * cols)
        arriving = lax.all_to_all(outgoing, PLANE, 0, 0, tiled=True)

    with jax.named_scope("gate"):
        gain = norm_gain.astype(F32)[None, :]
        router = lax.dynamic_index_in_dim(router_weight, yl, 1, False).astype(F32)[None, :]
        slots = seqs * 2 * CAP
        *routed, hidden = pl.pallas_call(
            gate_kernel,
            out_shape=[jax.ShapeDtypeStruct((slots // 2, model), BF16)] * 2
            + [jax.ShapeDtypeStruct((experts // 2, slots, cols), BF16)],
            in_specs=[vmem] * 3,
            out_specs=[vmem] * 3,
            compiler_params=pltpu.CompilerParams(vmem_limit_bytes=24 << 20),
        )(arriving, gain, router)

    with jax.named_scope("weight_swap"):
        given = after(1 - yl, outgoing)
        down_got = lax.ppermute(pick_expert(down_weight, given), "yl", swap)
        rest_got = lax.ppermute(pick_expert(up_weight[:, upper:], given), "yl", swap)
        gate_own, up_own, down_own = (
            pick_expert(w, yl) for w in (gate_weight, up_weight, down_weight)
        )
    weights = (gate_own, up_own, down_own, first_got, rest_got, down_got)

    with jax.named_scope("experts"):
        up_send, down_send = ring(nz, 1), ring(nz, -1)
        up, down = [list(routed)], [list(routed)]
        for k in range(1, nz // 2):
            pairs = []
            for h in range(2):
                pair = (
                    lax.ppermute(up[-1][h], "z", up_send),
                    lax.ppermute(down[-1][h], "z", down_send),
                )
                pairs.append(lax.optimization_barrier(pair))
            up.append([pair[0] for pair in pairs])
            down.append([pair[1] for pair in pairs])
        far = [
            lax.ppermute(up[-1][0], "z", up_send),
            lax.ppermute(down[-1][1], "z", down_send),
        ]
        outs = run_experts([t for pair in (*up, *down[1:], far) for t in pair], weights)
        outs = [list(outs[i : i + 2]) for i in range(0, len(outs), 2)]
        from_below, from_above = outs[: nz // 2], [None, *outs[nz // 2 : -1]]
        own, far = from_below[0], outs[-1]

        def move(a, b):
            return lax.ppermute(a, "z", up_send), lax.ppermute(b, "z", down_send)

        long, short = move(*far), None
        for k in range(nz // 2 - 1, 0, -1):
            if short is None:
                short = move(from_above[k][1], from_below[k][0])
            else:
                short = move(*add_pair(short[0], from_above[k][1], short[1], from_below[k][0]))
            long = move(*add_pair(long[0], from_above[k][0], long[1], from_below[k][1]))
        up_sum, down_sum = (long[0], short[0]), (short[1], long[1])

    with jax.named_scope("return"):
        lead = hidden.reshape(experts, slots // 2, cols)
        back = pl.pallas_call(
            finish_kernel,
            out_shape=jax.ShapeDtypeStruct((experts, slots // 2, cols), BF16),
            in_specs=[vmem] * 7,
            out_specs=vmem,
            compiler_params=pltpu.CompilerParams(vmem_limit_bytes=24 << 20),
        )(*own, *up_sum, *down_sum, lead)
        back = lax.all_to_all(back, PLANE, 0, 0, tiled=True)
        back = back.reshape(-1, cols)
        return jnp.dot(put, back, preferred_element_type=F32).astype(BF16).reshape(seqs, rows, cols)


def solution(mesh):
    fine = Mesh(mesh.devices.reshape(8, 2, 4, 2, 2), ("z", "yl", "x", "yh", "c"))
    ctx = ("z", "yl")
    in_specs = (
        P(E_AXES, ctx, None),
        P(E_AXES, ctx, None),
        P(E_AXES, ctx, None),
        P(E_AXES, ctx, None),
        P(E_AXES, ctx, None),
        P(E_AXES),
        P(None, ctx, E_AXES),
        P(None, E_AXES),
        P(),
        P(None, E_AXES),
        P(),
        P(E_AXES, None, ctx),
        P(E_AXES, None, ctx),
        P(E_AXES, ctx, None),
    )
    out_specs = P(None, ctx, E_AXES)
    return jax.shard_map(
        per_device, mesh=fine, in_specs=in_specs, out_specs=out_specs, check_vma=False
    )
```

```python
import functools
import math

import jax
import jax.numpy as jnp
from jax import lax
from jax.experimental import pallas as pl
from jax.experimental.pallas import tpu as pltpu
from jax.sharding import Mesh, PartitionSpec as P

HEADS = 20
KV_HEADS = 4
HEAD_DIM = 128
GROUP = HEADS // KV_HEADS
CAP = 3
EPSILON = 1e-05
FAR = 1 << 30
FILL = -1e30
LOW = -1e20
E_AXES = ("x", "yh", "c")
PLANE = ("x", "yh", "c", "yl")
F32 = jnp.float32
BF16 = jnp.bfloat16


def attend_kernel(pieces, first, last, *refs):
    q_ref, place_ref = refs[0], refs[1]
    key_refs = refs[2 : 2 + pieces]
    value_refs = refs[2 + pieces : 2 + 2 * pieces]
    rest = refs[2 + 2 * pieces :]
    if not first:
        held = rest[0]
        rest = rest[1:]
    rows = q_ref.shape[0]
    pair = q_ref.shape[1] // (GROUP * HEAD_DIM)
    factor = math.log2(math.e) / math.sqrt(HEAD_DIM)
    own = lax.broadcasted_iota(jnp.int32, (GROUP * rows, 1), 0) % rows
    for j in range(pair):
        queries = jnp.concatenate(
            [
                q_ref[:, (j * GROUP + g) * HEAD_DIM : (j * GROUP + g + 1) * HEAD_DIM]
                for g in range(GROUP)
            ],
            axis=0,
        )
        lanes = slice(j * HEAD_DIM, (j + 1) * HEAD_DIM)
        scores = []
        for i in range(pieces):
            s = lax.dot_general(
                queries,
                key_refs[i][:, lanes],
                (((1,), (1,)), ((), ())),
                preferred_element_type=F32,
            )
            scores.append(jnp.where(place_ref[i] <= own, s * factor, FILL))
        top = functools.reduce(
            jnp.maximum, [jnp.max(s, axis=-1, keepdims=True) for s in scores]
        )
        if first:
            high = jnp.maximum(top, LOW)
        else:
            m_old = held[j, :, HEAD_DIM : HEAD_DIM + 1]
            high = jnp.maximum(m_old, top)
            alpha = jnp.exp2(m_old - high)
        total = 0.0
        summed = 0.0
        for i in range(pieces):
            p = jnp.exp2(scores[i] - high)
            total = total + jnp.sum(p, axis=-1, keepdims=True)
            summed = summed + jnp.dot(
                p.astype(BF16), value_refs[i][:, lanes], preferred_element_type=F32
            )
        if not first:
            total = held[j, :, 3 * HEAD_DIM // 2 : 3 * HEAD_DIM // 2 + 1] * alpha + total
            summed = held[j, :, :HEAD_DIM] * alpha + summed
        if last:
            result = (summed / total).astype(BF16)
            for g in range(GROUP):
                rest[0][:, (j * GROUP + g) * HEAD_DIM : (j * GROUP + g + 1) * HEAD_DIM] = result[
                    g * rows : (g + 1) * rows
                ]
        else:
            lane = lax.broadcasted_iota(jnp.int32, (GROUP * rows, HEAD_DIM), 1)
            rest[0][j, :, :HEAD_DIM] = summed
            rest[0][j, :, HEAD_DIM:] = jnp.where(lane < HEAD_DIM // 2, high, total)


def attend(queries, places, keys, values, state, last):
    pieces = len(keys)
    rows, width = queries.shape
    pair = width // (GROUP * HEAD_DIM)
    stat = jax.ShapeDtypeStruct((pair, GROUP * rows, 2 * HEAD_DIM), F32)
    out = jax.ShapeDtypeStruct((rows, width), BF16) if last else stat
    keys_total = sum(k.shape[0] for k in keys)
    work = pair * GROUP * rows * keys_total
    vmem = pl.BlockSpec(memory_space=pltpu.VMEM)
    return pl.pallas_call(
        functools.partial(attend_kernel, pieces, state is None, last),
        out_shape=out,
        in_specs=[vmem] * (2 + 2 * pieces + (0 if state is None else 1)),
        out_specs=vmem,
        compiler_params=pltpu.CompilerParams(vmem_limit_bytes=24 << 20),
        cost_estimate=pl.CostEstimate(
            flops=16 * 4 * work * HEAD_DIM,
            bytes_accessed=4 * keys_total * pair * HEAD_DIM + 2 * 4 * stat.size,
            transcendentals=work,
        ),
    )(queries, places, *keys, *values, *(() if state is None else (state,)))


def project_kernel(own, other, far_own, far_other, weight, residual, pick, token, outgoing):
    del token
    half = own.shape[1]
    c = lax.axis_index("c")
    yh = lax.axis_index("yh")
    near_w = weight[:, pl.ds(pl.multiple_of(c * half, half), half)]
    far_w = weight[:, pl.ds(pl.multiple_of((1 - c) * half, half), half)]
    near_x = jnp.concatenate([own[...], other[...]], axis=0)
    far_x = jnp.concatenate([far_own[...], far_other[...]], axis=0)
    across = (((1,), (1,)), ((), ()))
    projected = lax.dot_general(near_x, near_w, across, preferred_element_type=F32)
    projected += lax.dot_general(far_x, far_w, across, preferred_element_type=F32)
    lead = jnp.concatenate(
        [
            jnp.concatenate(
                [residual[x * 2 + block, turn].astype(F32) for turn in (yh, 1 - yh) for block in range(2)],
                axis=0,
            )
            for x in range(residual.shape[0] // 2)
        ],
        axis=1,
    )
    hidden = (lead + projected).astype(BF16)
    outgoing[...] = jnp.dot(pick[...], hidden, preferred_element_type=F32).astype(BF16)


def gate_kernel(arriving, gain, router, first, second, rows_out):
    slots = first.shape[0] + second.shape[0]
    sources = arriving.shape[0] // 4
    room = arriving.shape[1]
    row = lax.broadcasted_iota(jnp.int32, (slots, sources * room), 0)
    wanted = lax.broadcasted_iota(jnp.int32, (slots, sources * room), 1)
    rank = row % CAP
    seq = row // CAP % 8 + row // (16 * CAP) * 8
    block = row // (8 * CAP) % 2
    source = (seq // 4 * 2 + seq % 2) * room + seq // 2 % 2 * 8 + block * 4 + rank
    compact = jnp.where(source == wanted, 1.0, 0.0).astype(BF16)
    groups = []
    for g in range(4):
        yh, c = g // 2, g % 2
        stacked = jnp.concatenate(
            [arriving[((x * 2 + yh) * 2 + c) * 2 + yl] for x in range(sources // 2) for yl in range(2)],
            axis=0,
        )
        groups.append(jnp.dot(compact, stacked, preferred_element_type=F32))
    cols = rows_out.shape[2]
    pieces = [
        groups[piece % 4][:, piece // 4 * cols : (piece // 4 + 1) * cols]
        for piece in range(rows_out.shape[0])
    ]
    numbers = jnp.concatenate(pieces, axis=1)
    step = slots // 4
    for i, piece in enumerate(pieces):
        rows_out[i] = jnp.concatenate(
            [piece[q * step : (q + 1) * step] for q in (0, 2, 1, 3)], axis=0
        ).astype(BF16)
    mean_square = jnp.mean(numbers * numbers, axis=-1, keepdims=True)
    normed = numbers * lax.rsqrt(mean_square + EPSILON) * gain[...]
    logits = jnp.sum(normed * router[...], axis=-1, keepdims=True)
    routed = (normed / (1.0 + jnp.exp(-logits))).astype(BF16)
    first[...] = routed[: slots // 2]
    second[...] = routed[slots // 2 :]


def finish_kernel(own_a, own_b, up_a, up_b, down_a, down_b, lead, out):
    halves = []
    for own, up, down in ((own_a, up_a, down_a), (own_b, up_b, down_b)):
        total = own[...].astype(F32) + up[...].astype(F32) + down[...].astype(F32)
        halves.append(total.astype(BF16).astype(F32))
    step = halves[0].shape[0] // 2
    cols = out.shape[2]
    for block in range(2):
        rows = jnp.concatenate([h[block * step : (block + 1) * step] for h in halves], axis=0)
        for piece in range(out.shape[0] // 2):
            add = lead[piece * 2 + block].astype(F32)
            out[piece * 2 + block] = (
                rows[:, piece * cols : (piece + 1) * cols] + add
            ).astype(BF16)


def add_kernel(a, b, c, d, first, second):
    first[...] = (a[...].astype(F32) + b[...].astype(F32)).astype(BF16)
    second[...] = (c[...].astype(F32) + d[...].astype(F32)).astype(BF16)


def add_pair(a, b, c, d):
    vmem = pl.BlockSpec(memory_space=pltpu.VMEM)
    return pl.pallas_call(
        add_kernel,
        out_shape=[jax.ShapeDtypeStruct(a.shape, BF16)] * 2,
        in_specs=[vmem] * 4,
        out_specs=[vmem] * 2,
        compiler_params=pltpu.CompilerParams(vmem_limit_bytes=8 << 20),
        cost_estimate=pl.CostEstimate(
            flops=2 * a.size, bytes_accessed=12 * a.size, transcendentals=0
        ),
    )(a, b, c, d)


def expert_kernel(pieces, *refs):
    token_refs = refs[:pieces]
    gate_own, up_own, down_own, first_got, rest_got, down_got = refs[pieces : pieces + 6]
    outs = refs[pieces + 6 :]
    model = gate_own.shape[0]
    upper = first_got.shape[0] - model
    sides = (
        (gate_own, ((up_own, 0, model),), down_own),
        (
            first_got.at[pl.ds(0, model)],
            ((first_got.at[pl.ds(model, upper)], 0, upper), (rest_got, upper, model)),
            down_got,
        ),
    )
    rows = token_refs[0].shape[0]
    for at in range(0, pieces, 8):
        tokens = jnp.concatenate([t[...] for t in token_refs[at : at + 8]], axis=0)
        total = 0.0
        for gate_w, up_parts, down_w in sides:
            g = jnp.dot(tokens, gate_w[...], preferred_element_type=F32)
            u = sum(
                jnp.dot(tokens[:, lo:hi], part[...], preferred_element_type=F32)
                for part, lo, hi in up_parts
            )
            a = (g / (1.0 + jnp.exp(-g)) * u).astype(BF16)
            total = total + jnp.dot(a, down_w[...], preferred_element_type=F32)
        total = total.astype(BF16)
        for i, out in enumerate(outs[at : at + 8]):
            out[...] = total[i * rows : (i + 1) * rows]


def run_experts(tokens, weights):
    pieces = len(tokens)
    rows, model = tokens[0].shape
    vmem = pl.BlockSpec(memory_space=pltpu.VMEM)
    size = sum(w.size for w in weights)
    return pl.pallas_call(
        functools.partial(expert_kernel, pieces),
        out_shape=[jax.ShapeDtypeStruct((rows, model), BF16)] * pieces,
        in_specs=[vmem] * (pieces + 6),
        out_specs=[vmem] * pieces,
        compiler_params=pltpu.CompilerParams(vmem_limit_bytes=36 << 20),
        cost_estimate=pl.CostEstimate(
            flops=5 * 2 * pieces * rows * size,
            bytes_accessed=2 * size + 4 * pieces * rows * model,
            transcendentals=pieces * rows * 512,
        ),
    )(*tokens, *weights)


def in_block_ranks(ids, block_rows):
    count = ids.shape[0]
    row = jnp.arange(count, dtype=jnp.int32)
    same = ids[:, None] == ids[None, :]
    before = (row[None, :] < row[:, None]) & (
        row[None, :] // block_rows == row[:, None] // block_rows
    )
    return jnp.sum((same & before).astype(jnp.int32), axis=-1)


def after(small, *arrays):
    for array in arrays:
        corner = lax.slice(array, (0,) * array.ndim, (1,) * array.ndim).reshape(())
        small, corner = lax.optimization_barrier((small, corner))
        small = jnp.maximum(small, jnp.where(corner != corner, small, small - 1))
    return small


def ring(size, step):
    return [(i, (i + step) % size) for i in range(size)]


def per_device(
    query_rows,
    stretch_keys,
    stretch_values,
    cache_keys,
    cache_values,
    cache_len,
    residual,
    out_weight,
    norm_gain,
    router_weight,
    expert_ids,
    gate_weight,
    up_weight,
    down_weight,
):
    z = lax.axis_index("z")
    yl = lax.axis_index("yl")
    x = lax.axis_index("x")
    yh = lax.axis_index("yh")
    c = lax.axis_index("c")
    nz = lax.axis_size("z")
    nx = lax.axis_size("x")
    rows = query_rows.shape[1]
    cache_rows = cache_keys.shape[1]
    width = query_rows.shape[2]
    half = width // 2
    kv_width = cache_keys.shape[2]
    kv_half = kv_width // 2
    seqs = residual.shape[0]
    cols = residual.shape[2]
    model = cols * lax.axis_size(E_AXES)
    experts = gate_weight.shape[0] * lax.axis_size(E_AXES)

    first_half = yl
    keys_own = jnp.concatenate([cache_keys[0], stretch_keys[0]], axis=0)
    values_own = jnp.concatenate([cache_values[0], stretch_values[0]], axis=0)

    def lanes(array, h, size):
        return lax.dynamic_slice_in_dim(array, h * size, size, 1)

    def keys_and_values(h):
        return jnp.concatenate(
            [lanes(keys_own, h, kv_half), lanes(values_own, h, kv_half)], axis=1
        )

    straight = [(y * 2 + k, k * 2 + y) for y in range(2) for k in range(2)]
    crossed = [(y * 2 + k, k * 2 + 1 - y) for y in range(2) for k in range(2)]

    def send(part):
        a = lax.ppermute(part(first_half), ("yl", "c"), straight)
        b = lax.ppermute(part(1 - first_half), ("yl", "c"), crossed)
        return a, b

    def join(a, b):
        return jnp.concatenate([jnp.where(c == 0, a, b), jnp.where(c == 0, b, a)], axis=0)

    with jax.named_scope("to_chip"):
        kv_parts = send(keys_and_values)
        query_parts = send(lambda h: lanes(query_rows[0], after(h, kv_parts[0]), half))
        keys0 = join(*(p[:, :kv_half] for p in kv_parts))
        values0 = join(*(p[:, kv_half:] for p in kv_parts))
        queries = join(*query_parts)
        length = lax.ppermute(
            jnp.broadcast_to(cache_len.astype(F32), (8, 128)), ("yl", "c"), straight
        )[0, 0].astype(jnp.int32)

    with jax.named_scope("out_weight_gather"):
        weight_cols = lax.all_gather(out_weight.T, "x", axis=0, tiled=True)

    def pick_expert(array, index):
        return lax.dynamic_index_in_dim(array, index, 0, False)

    with jax.named_scope("weight_swap"):
        swap = [(0, 1), (1, 0)]
        given = after(1 - yl, *query_parts)
        upper = model * 3 // 4
        first_got = lax.ppermute(
            jnp.concatenate(
                [pick_expert(gate_weight, given), pick_expert(up_weight[:, :upper], given)], axis=0
            ),
            "yl",
            swap,
        )

    ids = expert_ids[..., 0].reshape(nx, 2, 2, nz, 2, rows)

    with jax.named_scope("slots"):
        here = lax.dynamic_index_in_dim(ids, z, 3, False)
        source_ids = lax.dynamic_index_in_dim(here, x, 0, False)
        source_ids = lax.dynamic_index_in_dim(source_ids, yl, 1, False)
        source_ids = jnp.where(yh == 0, source_ids, source_ids[::-1]).reshape(4 * rows)
        ranks = in_block_ranks(source_ids, rows)
        wanted = jnp.arange(experts * 16, dtype=jnp.int32)
        wanted_expert = wanted // 16
        wanted_block = wanted // 4 % 4
        wanted_rank = wanted % 4
        row_block = jnp.arange(4 * rows, dtype=jnp.int32) // rows ^ (yh * 2)
        pick = (
            (wanted_expert[:, None] == source_ids[None, :])
            & (wanted_rank[:, None] == ranks[None, :])
            & (wanted_block[:, None] == row_block[None, :])
        ).astype(BF16)
        same = lax.dynamic_index_in_dim(here, yl, 3, False).reshape(seqs, rows)
        earlier = jnp.arange(rows)[None, :] < jnp.arange(rows)[:, None]
        home_ranks = jnp.sum(
            ((same[:, :, None] == same[:, None, :]) & earlier[None]).astype(jnp.int32), axis=-1
        )
        code = (same * seqs + jnp.arange(seqs)[:, None]) * CAP + home_ranks
        table = jnp.arange(experts * seqs * CAP, dtype=jnp.int32)
        put = (code.reshape(seqs * rows, 1) == table).astype(BF16)

    span = rows + cache_rows

    def places(offset):
        holder = (z + offset) % nz
        r = jnp.arange(2 * span, dtype=jnp.int32)
        block, within = r // span, r % span
        slot = (holder * 2 + block) * cache_rows + within
        stretch = ((holder - z) * 2 + block) * rows + within - cache_rows
        return jnp.where(
            within < cache_rows, jnp.where(slot < length, -FAR, FAR), stretch
        )[None, :]

    with jax.named_scope("attention"):
        up_k, up_v, down_k, down_v = keys0, values0, keys0, values0
        state = None
        for step in range(1, nz // 2):
            up_k = lax.ppermute(up_k, "z", ring(nz, 1))
            down_k = lax.ppermute(down_k, "z", ring(nz, -1))
            up_v = lax.ppermute(up_v, "z", ring(nz, 1))
            down_v = lax.ppermute(down_v, "z", ring(nz, -1))
            step_keys, step_values = [up_k, down_k], [up_v, down_v]
            step_places = [places(-step), places(step)]
            if step == 2:
                corner, residual = lax.optimization_barrier((step_corner, residual))
            if step == 1:
                step_corner = up_k[:1, :1]
                step_keys.append(keys0)
                step_values.append(values0)
                step_places.append(places(0))
            state = attend(
                queries, jnp.stack(step_places), step_keys, step_values, state, False
            )
        far_k = lax.ppermute(up_k, "z", ring(nz, 1))
        far_v = lax.ppermute(down_v, "z", ring(nz, -1))
        last_places = places(nz // 2)
        attended = attend(
            queries,
            jnp.stack([jnp.maximum(last_places, jnp.where(corner != corner, last_places, last_places - 1))]),
            [far_k],
            [far_v],
            state,
            True,
        )

    vmem = pl.BlockSpec(memory_space=pltpu.VMEM)

    with jax.named_scope("out_projection"):
        other = lax.ppermute(attended, "yh", swap)
        far_own = lax.ppermute(attended, "c", swap)
        far_other = lax.ppermute(other, "c", swap)
        moved = residual.reshape(nx, 2, 2, rows, cols).transpose(0, 2, 1, 3, 4)
        moved = moved.reshape(nx * 2, 2, rows, cols)
        residual_rows = lax.all_to_all(moved, ("x", "yl"), 0, 0, tiled=True)
        outgoing = pl.pallas_call(
            project_kernel,
            out_shape=jax.ShapeDtypeStruct((experts * 16, nx * cols), BF16),
            in_specs=[vmem] * 8,
            out_specs=vmem,
            compiler_params=pltpu.CompilerParams(vmem_limit_bytes=24 << 20),
        )(
            attended,
            other,
            far_own,
            far_other,
            weight_cols,
            residual_rows,
            pick,
            first_got[:16, :128],
        )

    with jax.named_scope("dispatch"):
        outgoing = outgoing.reshape(experts, 16, nx * cols)
        arriving = lax.all_to_all(outgoing, PLANE, 0, 0, tiled=True)

    with jax.named_scope("gate"):
        gain = norm_gain.astype(F32)[None, :]
        router = lax.dynamic_index_in_dim(router_weight, yl, 1, False).astype(F32)[None, :]
        slots = seqs * 2 * CAP
        *routed, hidden = pl.pallas_call(
            gate_kernel,
            out_shape=[jax.ShapeDtypeStruct((slots // 2, model), BF16)] * 2
            + [jax.ShapeDtypeStruct((experts // 2, slots, cols), BF16)],
            in_specs=[vmem] * 3,
            out_specs=[vmem] * 3,
            compiler_params=pltpu.CompilerParams(vmem_limit_bytes=24 << 20),
        )(arriving, gain, router)

    with jax.named_scope("weight_swap"):
        given = after(1 - yl, outgoing)
        down_got = lax.ppermute(pick_expert(down_weight, given), "yl", swap)
        rest_got = lax.ppermute(pick_expert(up_weight[:, upper:], given), "yl", swap)
        gate_own, up_own, down_own = (
            pick_expert(w, yl) for w in (gate_weight, up_weight, down_weight)
        )
    weights = (gate_own, up_own, down_own, first_got, rest_got, down_got)

    with jax.named_scope("experts"):
        up_send, down_send = ring(nz, 1), ring(nz, -1)
        up, down = [list(routed)], [list(routed)]
        for k in range(1, nz // 2):
            pairs = []
            for h in range(2):
                pair = (
                    lax.ppermute(up[-1][h], "z", up_send),
                    lax.ppermute(down[-1][h], "z", down_send),
                )
                pairs.append(lax.optimization_barrier(pair))
            up.append([pair[0] for pair in pairs])
            down.append([pair[1] for pair in pairs])
        far = [
            lax.ppermute(up[-1][0], "z", up_send),
            lax.ppermute(down[-1][1], "z", down_send),
        ]
        outs = run_experts([t for pair in (*up, *down[1:], far) for t in pair], weights)
        outs = [list(outs[i : i + 2]) for i in range(0, len(outs), 2)]
        from_below, from_above = outs[: nz // 2], [None, *outs[nz // 2 : -1]]
        own, far = from_below[0], outs[-1]

        def move(a, b):
            return lax.ppermute(a, "z", up_send), lax.ppermute(b, "z", down_send)

        long, short = move(*far), None
        for k in range(nz // 2 - 1, 0, -1):
            if short is None:
                short = move(from_above[k][1], from_below[k][0])
            else:
                short = move(*add_pair(short[0], from_above[k][1], short[1], from_below[k][0]))
            long = move(*add_pair(long[0], from_above[k][0], long[1], from_below[k][1]))
        up_sum, down_sum = (long[0], short[0]), (short[1], long[1])

    with jax.named_scope("return"):
        lead = hidden.reshape(experts, slots // 2, cols)
        back = pl.pallas_call(
            finish_kernel,
            out_shape=jax.ShapeDtypeStruct((experts, slots // 2, cols), BF16),
            in_specs=[vmem] * 7,
            out_specs=vmem,
            compiler_params=pltpu.CompilerParams(vmem_limit_bytes=24 << 20),
        )(*own, *up_sum, *down_sum, lead)
        back = lax.all_to_all(back, PLANE, 0, 0, tiled=True)
        back = back.reshape(-1, cols)
        return jnp.dot(put, back, preferred_element_type=F32).astype(BF16).reshape(seqs, rows, cols)


def solution(mesh):
    fine = Mesh(mesh.devices.reshape(8, 2, 4, 2, 2), ("z", "yl", "x", "yh", "c"))
    ctx = ("z", "yl")
    in_specs = (
        P(E_AXES, ctx, None),
        P(E_AXES, ctx, None),
        P(E_AXES, ctx, None),
        P(E_AXES, ctx, None),
        P(E_AXES, ctx, None),
        P(E_AXES),
        P(None, ctx, E_AXES),
        P(None, E_AXES),
        P(),
        P(None, E_AXES),
        P(),
        P(E_AXES, None, ctx),
        P(E_AXES, None, ctx),
        P(E_AXES, ctx, None),
    )
    out_specs = P(None, ctx, E_AXES)
    return jax.shard_map(
        per_device, mesh=fine, in_specs=in_specs, out_specs=out_specs, check_vma=False
    )
```

```python
import functools
import math

import jax
import jax.numpy as jnp
from jax import lax
from jax.experimental import pallas as pl
from jax.experimental.pallas import tpu as pltpu
from jax.sharding import Mesh, PartitionSpec as P

HEADS = 20
KV_HEADS = 4
HEAD_DIM = 128
GROUP = HEADS // KV_HEADS
CAP = 3
EPSILON = 1e-05
FAR = 1 << 30
FILL = -1e30
LOW = -1e20
E_AXES = ("x", "yh", "c")
PLANE = ("x", "yh", "c", "yl")
F32 = jnp.float32
BF16 = jnp.bfloat16


def attend_kernel(pieces, first, last, *refs):
    q_ref, place_ref = refs[0], refs[1]
    key_refs = refs[2 : 2 + pieces]
    value_refs = refs[2 + pieces : 2 + 2 * pieces]
    rest = refs[2 + 2 * pieces :]
    if not first:
        held = rest[0]
        rest = rest[1:]
    rows = q_ref.shape[0]
    pair = q_ref.shape[1] // (GROUP * HEAD_DIM)
    factor = math.log2(math.e) / math.sqrt(HEAD_DIM)
    own = lax.broadcasted_iota(jnp.int32, (GROUP * rows, 1), 0) % rows
    for j in range(pair):
        queries = jnp.concatenate(
            [
                q_ref[:, (j * GROUP + g) * HEAD_DIM : (j * GROUP + g + 1) * HEAD_DIM]
                for g in range(GROUP)
            ],
            axis=0,
        )
        lanes = slice(j * HEAD_DIM, (j + 1) * HEAD_DIM)
        scores = []
        for i in range(pieces):
            s = lax.dot_general(
                queries,
                key_refs[i][:, lanes],
                (((1,), (1,)), ((), ())),
                preferred_element_type=F32,
            )
            scores.append(jnp.where(place_ref[i] <= own, s * factor, FILL))
        top = functools.reduce(
            jnp.maximum, [jnp.max(s, axis=-1, keepdims=True) for s in scores]
        )
        if first:
            high = jnp.maximum(top, LOW)
        else:
            m_old = held[j, :, HEAD_DIM : HEAD_DIM + 1]
            high = jnp.maximum(m_old, top)
            alpha = jnp.exp2(m_old - high)
        total = 0.0
        summed = 0.0
        for i in range(pieces):
            p = jnp.exp2(scores[i] - high)
            total = total + jnp.sum(p, axis=-1, keepdims=True)
            summed = summed + jnp.dot(
                p.astype(BF16), value_refs[i][:, lanes], preferred_element_type=F32
            )
        if not first:
            total = held[j, :, 3 * HEAD_DIM // 2 : 3 * HEAD_DIM // 2 + 1] * alpha + total
            summed = held[j, :, :HEAD_DIM] * alpha + summed
        if last:
            result = (summed / total).astype(BF16)
            for g in range(GROUP):
                rest[0][:, (j * GROUP + g) * HEAD_DIM : (j * GROUP + g + 1) * HEAD_DIM] = result[
                    g * rows : (g + 1) * rows
                ]
        else:
            lane = lax.broadcasted_iota(jnp.int32, (GROUP * rows, HEAD_DIM), 1)
            rest[0][j, :, :HEAD_DIM] = summed
            rest[0][j, :, HEAD_DIM:] = jnp.where(lane < HEAD_DIM // 2, high, total)


def attend(queries, places, keys, values, state, last):
    pieces = len(keys)
    rows, width = queries.shape
    pair = width // (GROUP * HEAD_DIM)
    stat = jax.ShapeDtypeStruct((pair, GROUP * rows, 2 * HEAD_DIM), F32)
    out = jax.ShapeDtypeStruct((rows, width), BF16) if last else stat
    keys_total = sum(k.shape[0] for k in keys)
    work = pair * GROUP * rows * keys_total
    vmem = pl.BlockSpec(memory_space=pltpu.VMEM)
    return pl.pallas_call(
        functools.partial(attend_kernel, pieces, state is None, last),
        out_shape=out,
        in_specs=[vmem] * (2 + 2 * pieces + (0 if state is None else 1)),
        out_specs=vmem,
        compiler_params=pltpu.CompilerParams(vmem_limit_bytes=24 << 20),
        cost_estimate=pl.CostEstimate(
            flops=16 * 4 * work * HEAD_DIM,
            bytes_accessed=4 * keys_total * pair * HEAD_DIM + 2 * 4 * stat.size,
            transcendentals=work,
        ),
    )(queries, places, *keys, *values, *(() if state is None else (state,)))


def project_kernel(own, other, far_own, far_other, weight, residual, pick, token, outgoing):
    del token
    half = own.shape[1]
    c = lax.axis_index("c")
    yh = lax.axis_index("yh")
    near_w = weight[:, pl.ds(pl.multiple_of(c * half, half), half)]
    far_w = weight[:, pl.ds(pl.multiple_of((1 - c) * half, half), half)]
    near_x = jnp.concatenate([own[...], other[...]], axis=0)
    far_x = jnp.concatenate([far_own[...], far_other[...]], axis=0)
    across = (((1,), (1,)), ((), ()))
    projected = lax.dot_general(near_x, near_w, across, preferred_element_type=F32)
    projected += lax.dot_general(far_x, far_w, across, preferred_element_type=F32)
    lead = jnp.concatenate(
        [
            jnp.concatenate(
                [residual[x * 2 + block, turn].astype(F32) for turn in (yh, 1 - yh) for block in range(2)],
                axis=0,
            )
            for x in range(residual.shape[0] // 2)
        ],
        axis=1,
    )
    hidden = (lead + projected).astype(BF16)
    outgoing[...] = jnp.dot(pick[...], hidden, preferred_element_type=F32).astype(BF16)


def gate_kernel(arriving, gain, router, first, second, rows_out):
    slots = first.shape[0] + second.shape[0]
    sources = arriving.shape[0] // 4
    room = arriving.shape[1]
    row = lax.broadcasted_iota(jnp.int32, (slots, sources * room), 0)
    wanted = lax.broadcasted_iota(jnp.int32, (slots, sources * room), 1)
    rank = row % CAP
    seq = row // CAP % 8 + row // (16 * CAP) * 8
    block = row // (8 * CAP) % 2
    source = (seq // 4 * 2 + seq % 2) * room + seq // 2 % 2 * 8 + block * 4 + rank
    compact = jnp.where(source == wanted, 1.0, 0.0).astype(BF16)
    groups = []
    for g in range(4):
        yh, c = g // 2, g % 2
        stacked = jnp.concatenate(
            [arriving[((x * 2 + yh) * 2 + c) * 2 + yl] for x in range(sources // 2) for yl in range(2)],
            axis=0,
        )
        groups.append(jnp.dot(compact, stacked, preferred_element_type=F32))
    cols = rows_out.shape[2]
    pieces = [
        groups[piece % 4][:, piece // 4 * cols : (piece // 4 + 1) * cols]
        for piece in range(rows_out.shape[0])
    ]
    numbers = jnp.concatenate(pieces, axis=1)
    step = slots // 4
    for i, piece in enumerate(pieces):
        rows_out[i] = jnp.concatenate(
            [piece[q * step : (q + 1) * step] for q in (0, 2, 1, 3)], axis=0
        ).astype(BF16)
    mean_square = jnp.mean(numbers * numbers, axis=-1, keepdims=True)
    normed = numbers * lax.rsqrt(mean_square + EPSILON) * gain[...]
    logits = jnp.sum(normed * router[...], axis=-1, keepdims=True)
    routed = (normed / (1.0 + jnp.exp(-logits))).astype(BF16)
    first[...] = routed[: slots // 2]
    second[...] = routed[slots // 2 :]


def finish_kernel(own_a, own_b, up_a, up_b, down_a, down_b, lead, out):
    halves = []
    for own, up, down in ((own_a, up_a, down_a), (own_b, up_b, down_b)):
        total = own[...].astype(F32) + up[...].astype(F32) + down[...].astype(F32)
        halves.append(total.astype(BF16).astype(F32))
    step = halves[0].shape[0] // 2
    cols = out.shape[2]
    for block in range(2):
        rows = jnp.concatenate([h[block * step : (block + 1) * step] for h in halves], axis=0)
        for piece in range(out.shape[0] // 2):
            add = lead[piece * 2 + block].astype(F32)
            out[piece * 2 + block] = (
                rows[:, piece * cols : (piece + 1) * cols] + add
            ).astype(BF16)


def add_kernel(a, b, c, d, first, second):
    first[...] = (a[...].astype(F32) + b[...].astype(F32)).astype(BF16)
    second[...] = (c[...].astype(F32) + d[...].astype(F32)).astype(BF16)


def add_pair(a, b, c, d):
    vmem = pl.BlockSpec(memory_space=pltpu.VMEM)
    return pl.pallas_call(
        add_kernel,
        out_shape=[jax.ShapeDtypeStruct(a.shape, BF16)] * 2,
        in_specs=[vmem] * 4,
        out_specs=[vmem] * 2,
        compiler_params=pltpu.CompilerParams(vmem_limit_bytes=8 << 20),
        cost_estimate=pl.CostEstimate(
            flops=2 * a.size, bytes_accessed=12 * a.size, transcendentals=0
        ),
    )(a, b, c, d)


def expert_kernel(pieces, *refs):
    token_refs = refs[:pieces]
    gate_own, up_own, down_own, first_got, second_got = refs[pieces : pieces + 5]
    outs = refs[pieces + 5 :]
    model = gate_own.shape[0]
    upper = first_got.shape[0] - model
    sides = (
        (gate_own, ((up_own, 0, model),), down_own),
        (
            first_got.at[pl.ds(0, model)],
            ((first_got.at[pl.ds(model, upper)], 0, upper), (second_got.at[pl.ds(0, model - upper)], upper, model)),
            second_got.at[pl.ds(model - upper, model)],
        ),
    )
    rows = token_refs[0].shape[0]
    for at in range(0, pieces, 8):
        tokens = jnp.concatenate([t[...] for t in token_refs[at : at + 8]], axis=0)
        total = 0.0
        for gate_w, up_parts, down_w in sides:
            g = jnp.dot(tokens, gate_w[...], preferred_element_type=F32)
            u = sum(
                jnp.dot(tokens[:, lo:hi], part[...], preferred_element_type=F32)
                for part, lo, hi in up_parts
            )
            a = (g / (1.0 + jnp.exp(-g)) * u).astype(BF16)
            across = (((1,), (0 if down_w.shape[1] == model else 1,)), ((), ()))
            total = total + lax.dot_general(a, down_w[...], across, preferred_element_type=F32)
        total = total.astype(BF16)
        for i, out in enumerate(outs[at : at + 8]):
            out[...] = total[i * rows : (i + 1) * rows]


def run_experts(tokens, weights):
    pieces = len(tokens)
    rows, model = tokens[0].shape
    vmem = pl.BlockSpec(memory_space=pltpu.VMEM)
    size = sum(w.size for w in weights)
    return pl.pallas_call(
        functools.partial(expert_kernel, pieces),
        out_shape=[jax.ShapeDtypeStruct((rows, model), BF16)] * pieces,
        in_specs=[vmem] * (pieces + 5),
        out_specs=[vmem] * pieces,
        compiler_params=pltpu.CompilerParams(vmem_limit_bytes=36 << 20),
        cost_estimate=pl.CostEstimate(
            flops=5 * 2 * pieces * rows * size,
            bytes_accessed=2 * size + 4 * pieces * rows * model,
            transcendentals=pieces * rows * 512,
        ),
    )(*tokens, *weights)


def in_block_ranks(ids, block_rows):
    count = ids.shape[0]
    row = jnp.arange(count, dtype=jnp.int32)
    same = ids[:, None] == ids[None, :]
    before = (row[None, :] < row[:, None]) & (
        row[None, :] // block_rows == row[:, None] // block_rows
    )
    return jnp.sum((same & before).astype(jnp.int32), axis=-1)


def after(small, *arrays):
    for array in arrays:
        corner = lax.slice(array, (0,) * array.ndim, (1,) * array.ndim).reshape(())
        small, corner = lax.optimization_barrier((small, corner))
        small = jnp.maximum(small, jnp.where(corner != corner, small, small - 1))
    return small


def ring(size, step):
    return [(i, (i + step) % size) for i in range(size)]


def per_device(
    query_rows,
    stretch_keys,
    stretch_values,
    cache_keys,
    cache_values,
    cache_len,
    residual,
    out_weight,
    norm_gain,
    router_weight,
    expert_ids,
    gate_weight,
    up_weight,
    down_weight,
):
    z = lax.axis_index("z")
    yl = lax.axis_index("yl")
    x = lax.axis_index("x")
    yh = lax.axis_index("yh")
    c = lax.axis_index("c")
    nz = lax.axis_size("z")
    nx = lax.axis_size("x")
    rows = query_rows.shape[1]
    cache_rows = cache_keys.shape[1]
    width = query_rows.shape[2]
    half = width // 2
    kv_width = cache_keys.shape[2]
    kv_half = kv_width // 2
    seqs = residual.shape[0]
    cols = residual.shape[2]
    model = cols * lax.axis_size(E_AXES)
    experts = gate_weight.shape[0] * lax.axis_size(E_AXES)

    first_half = yl
    keys_own = jnp.concatenate([cache_keys[0], stretch_keys[0]], axis=0)
    values_own = jnp.concatenate([cache_values[0], stretch_values[0]], axis=0)

    def lanes(array, h, size):
        return lax.dynamic_slice_in_dim(array, h * size, size, 1)

    def keys_and_values(h):
        return jnp.concatenate(
            [lanes(keys_own, h, kv_half), lanes(values_own, h, kv_half)], axis=1
        )

    straight = [(y * 2 + k, k * 2 + y) for y in range(2) for k in range(2)]
    crossed = [(y * 2 + k, k * 2 + 1 - y) for y in range(2) for k in range(2)]

    def send(part):
        a = lax.ppermute(part(first_half), ("yl", "c"), straight)
        b = lax.ppermute(part(1 - first_half), ("yl", "c"), crossed)
        return a, b

    def join(a, b):
        return jnp.concatenate([jnp.where(c == 0, a, b), jnp.where(c == 0, b, a)], axis=0)

    with jax.named_scope("to_chip"):
        kv_parts = send(keys_and_values)
        query_parts = send(lambda h: lanes(query_rows[0], after(h, kv_parts[0]), half))
        held, residual = lax.optimization_barrier((query_parts[0], residual))
        query_parts = (held, query_parts[1])
        keys0 = join(*(p[:, :kv_half] for p in kv_parts))
        values0 = join(*(p[:, kv_half:] for p in kv_parts))
        queries = join(*query_parts)
        length = lax.ppermute(
            jnp.broadcast_to(cache_len.astype(F32), (8, 128)), ("yl", "c"), straight
        )[0, 0].astype(jnp.int32)

    with jax.named_scope("out_weight_gather"):
        weight_cols = lax.all_gather(out_weight.T, "x", axis=0, tiled=True)

    def pick_expert(array, index):
        return lax.dynamic_index_in_dim(array, index, 0, False)

    with jax.named_scope("weight_swap"):
        swap = [(0, 1), (1, 0)]
        given = after(1 - yl, *query_parts)
        upper = model // 2
        first_got = lax.ppermute(
            jnp.concatenate(
                [pick_expert(gate_weight, given), pick_expert(up_weight[:, :upper], given)], axis=0
            ),
            "yl",
            swap,
        )

    ids = expert_ids[..., 0].reshape(nx, 2, 2, nz, 2, rows)

    with jax.named_scope("slots"):
        here = lax.dynamic_index_in_dim(ids, z, 3, False)
        source_ids = lax.dynamic_index_in_dim(here, x, 0, False)
        source_ids = lax.dynamic_index_in_dim(source_ids, yl, 1, False)
        source_ids = jnp.where(yh == 0, source_ids, source_ids[::-1]).reshape(4 * rows)
        ranks = in_block_ranks(source_ids, rows)
        wanted = jnp.arange(experts * 16, dtype=jnp.int32)
        wanted_expert = wanted // 16
        wanted_block = wanted // 4 % 4
        wanted_rank = wanted % 4
        row_block = jnp.arange(4 * rows, dtype=jnp.int32) // rows ^ (yh * 2)
        pick = (
            (wanted_expert[:, None] == source_ids[None, :])
            & (wanted_rank[:, None] == ranks[None, :])
            & (wanted_block[:, None] == row_block[None, :])
        ).astype(BF16)
        same = lax.dynamic_index_in_dim(here, yl, 3, False).reshape(seqs, rows)
        earlier = jnp.arange(rows)[None, :] < jnp.arange(rows)[:, None]
        home_ranks = jnp.sum(
            ((same[:, :, None] == same[:, None, :]) & earlier[None]).astype(jnp.int32), axis=-1
        )
        code = (same * seqs + jnp.arange(seqs)[:, None]) * CAP + home_ranks
        table = jnp.arange(experts * seqs * CAP, dtype=jnp.int32)
        put = (code.reshape(seqs * rows, 1) == table).astype(BF16)

    span = rows + cache_rows

    def places(offset):
        holder = (z + offset) % nz
        r = jnp.arange(2 * span, dtype=jnp.int32)
        block, within = r // span, r % span
        slot = (holder * 2 + block) * cache_rows + within
        stretch = ((holder - z) * 2 + block) * rows + within - cache_rows
        return jnp.where(
            within < cache_rows, jnp.where(slot < length, -FAR, FAR), stretch
        )[None, :]

    with jax.named_scope("attention"):
        up_k, up_v, down_k, down_v = keys0, values0, keys0, values0
        state = None
        for step in range(1, nz // 2):
            up_k = lax.ppermute(up_k, "z", ring(nz, 1))
            down_k = lax.ppermute(down_k, "z", ring(nz, -1))
            up_v = lax.ppermute(up_v, "z", ring(nz, 1))
            down_v = lax.ppermute(down_v, "z", ring(nz, -1))
            step_keys, step_values = [up_k, down_k], [up_v, down_v]
            step_places = [places(-step), places(step)]
            if step == 1:
                step_keys.append(keys0)
                step_values.append(values0)
                step_places.append(places(0))
            state = attend(
                queries, jnp.stack(step_places), step_keys, step_values, state, False
            )
        far_k = lax.ppermute(up_k, "z", ring(nz, 1))
        far_v = lax.ppermute(down_v, "z", ring(nz, -1))
        attended = attend(
            queries,
            jnp.stack([places(nz // 2)]),
            [far_k],
            [far_v],
            state,
            True,
        )

    vmem = pl.BlockSpec(memory_space=pltpu.VMEM)

    with jax.named_scope("out_projection"):
        other = lax.ppermute(attended, "yh", swap)
        far_own = lax.ppermute(attended, "c", swap)
        far_other = lax.ppermute(other, "c", swap)
        moved = residual.reshape(nx, 2, 2, rows, cols).transpose(0, 2, 1, 3, 4)
        moved = moved.reshape(nx * 2, 2, rows, cols)
        residual_rows = lax.all_to_all(moved, ("x", "yl"), 0, 0, tiled=True)
        outgoing = pl.pallas_call(
            project_kernel,
            out_shape=jax.ShapeDtypeStruct((experts * 16, nx * cols), BF16),
            in_specs=[vmem] * 8,
            out_specs=vmem,
            compiler_params=pltpu.CompilerParams(vmem_limit_bytes=24 << 20),
        )(
            attended,
            other,
            far_own,
            far_other,
            weight_cols,
            residual_rows,
            pick,
            first_got[:16, :128],
        )

    with jax.named_scope("dispatch"):
        outgoing = outgoing.reshape(experts, 16, nx * cols)
        arriving = lax.all_to_all(outgoing, PLANE, 0, 0, tiled=True)

    with jax.named_scope("gate"):
        gain = norm_gain.astype(F32)[None, :]
        router = lax.dynamic_index_in_dim(router_weight, yl, 1, False).astype(F32)[None, :]
        slots = seqs * 2 * CAP
        *routed, hidden = pl.pallas_call(
            gate_kernel,
            out_shape=[jax.ShapeDtypeStruct((slots // 2, model), BF16)] * 2
            + [jax.ShapeDtypeStruct((experts // 2, slots, cols), BF16)],
            in_specs=[vmem] * 3,
            out_specs=[vmem] * 3,
            compiler_params=pltpu.CompilerParams(vmem_limit_bytes=24 << 20),
        )(arriving, gain, router)

    with jax.named_scope("weight_swap"):
        given = after(1 - yl, outgoing)
        second_got = lax.ppermute(
            jnp.concatenate(
                [pick_expert(up_weight[:, upper:], given), pick_expert(down_weight, given).T], axis=0
            ),
            "yl",
            swap,
        )
        gate_own, up_own, down_own = (
            pick_expert(w, yl) for w in (gate_weight, up_weight, down_weight)
        )
    weights = (gate_own, up_own, down_own, first_got, second_got)

    with jax.named_scope("experts"):
        up_send, down_send = ring(nz, 1), ring(nz, -1)
        up, down = [list(routed)], [list(routed)]
        for k in range(1, nz // 2):
            pairs = []
            for h in range(2):
                pair = (
                    lax.ppermute(up[-1][h], "z", up_send),
                    lax.ppermute(down[-1][h], "z", down_send),
                )
                pairs.append(lax.optimization_barrier(pair))
            up.append([pair[0] for pair in pairs])
            down.append([pair[1] for pair in pairs])
        far = [
            lax.ppermute(up[-1][0], "z", up_send),
            lax.ppermute(down[-1][1], "z", down_send),
        ]
        outs = run_experts([t for pair in (*up, *down[1:], far) for t in pair], weights)
        outs = [list(outs[i : i + 2]) for i in range(0, len(outs), 2)]
        from_below, from_above = outs[: nz // 2], [None, *outs[nz // 2 : -1]]
        own, far = from_below[0], outs[-1]

        def move(a, b):
            return lax.ppermute(a, "z", up_send), lax.ppermute(b, "z", down_send)

        long, short = move(*far), None
        for k in range(nz // 2 - 1, 0, -1):
            if short is None:
                short = move(from_above[k][1], from_below[k][0])
            else:
                short = move(*add_pair(short[0], from_above[k][1], short[1], from_below[k][0]))
            long = move(*add_pair(long[0], from_above[k][0], long[1], from_below[k][1]))
        up_sum, down_sum = (long[0], short[0]), (short[1], long[1])

    with jax.named_scope("return"):
        lead = hidden.reshape(experts, slots // 2, cols)
        back = pl.pallas_call(
            finish_kernel,
            out_shape=jax.ShapeDtypeStruct((experts, slots // 2, cols), BF16),
            in_specs=[vmem] * 7,
            out_specs=vmem,
            compiler_params=pltpu.CompilerParams(vmem_limit_bytes=24 << 20),
        )(*own, *up_sum, *down_sum, lead)
        back = lax.all_to_all(back, PLANE, 0, 0, tiled=True)
        back = back.reshape(-1, cols)
        return jnp.dot(put, back, preferred_element_type=F32).astype(BF16).reshape(seqs, rows, cols)


def solution(mesh):
    fine = Mesh(mesh.devices.reshape(8, 2, 4, 2, 2), ("z", "yl", "x", "yh", "c"))
    ctx = ("z", "yl")
    in_specs = (
        P(E_AXES, ctx, None),
        P(E_AXES, ctx, None),
        P(E_AXES, ctx, None),
        P(E_AXES, ctx, None),
        P(E_AXES, ctx, None),
        P(E_AXES),
        P(None, ctx, E_AXES),
        P(None, E_AXES),
        P(),
        P(None, E_AXES),
        P(),
        P(E_AXES, None, ctx),
        P(E_AXES, None, ctx),
        P(E_AXES, ctx, None),
    )
    out_specs = P(None, ctx, E_AXES)
    return jax.shard_map(
        per_device, mesh=fine, in_specs=in_specs, out_specs=out_specs, check_vma=False
    )
```
